32 devices in a mesh: groups: 2 (over y), ctx: 8 (over z, x), batch: 2 (over core).
Axes of the slice: x: 2, y: 2, z: 4, core: 2. Of those that a mesh axis runs over, the one named last changes fastest.
Arguments:
- q_latent: bfloat16 [4, 64, 128, 576], P(('groups', 'batch'), 'ctx'), parts along dimension 0
- kv_new: bfloat16 [4, 64, 576], P(('groups', 'batch'), 'ctx'), parts along dimension 0
- kv_cache: bfloat16 [4, 1024, 576], P(('groups', 'batch'), 'ctx'), parts along dimension 0, may hold values from -6 to 6
- index_q: bfloat16 [4, 64, 64, 128], P(('groups', 'batch'), 'ctx'), parts along dimension 0, may hold values from -0.59765625 to 0.59765625
- index_weight: bfloat16 [4, 64, 64], P(('groups', 'batch'), 'ctx'), parts along dimension 0, may hold values from -3 to 3
- index_keys: bfloat16 [4, 1024, 128], P(('groups', 'batch'), 'ctx'), parts along dimension 0, may hold values from -6 to 6
- block_list: int32 [4, 8, 4], P(('groups', 'batch'), 'ctx'), parts along dimension 0, may hold values from 0 to 15, as said below
- context_len: int32 [4], P(('groups', 'batch')), parts along dimension 0, may hold values from 512 to 1024, as said below
Outputs:
- attended: bfloat16 [4, 64, 128, 512], P(('groups', 'batch'), 'ctx'), parts along dimension 0
- block_score: float32 [4, 64, 16], P(('groups', 'batch'), 'ctx'), parts along dimension 0
The draws below stay inside these ranges and needn't reach their ends.
There are 2 independent parts, one for each index of `groups`. The reference program is written for one: setup_inputs(seed, part) draws one part's arguments, and reference() takes and returns one part's arrays. A program takes and returns all parts, laid end to end along the dimension named above; each array names one. Nothing has to cross between parts.
Inputs may be any that keep to these rules, and one draw needn't show every extreme that they name: `block_list`: each entry is a page of the session's cache that starts below context_len; the 4 pages of one query tile are held by 4 different indices of ctx (page b by index b // 2). `context_len`: session 0 of every part has all 1024 cached tokens valid.
All inputs are finite; a program needn't handle non-finite values.
Results may differ from the reference program's by a relative error of at most 0.0035.
Values may be sent and summed in bfloat16 or wider, within the bound.
No kernel may reach another device: no remote copies, remote signals or barrier semaphores. Data moves between devices by JAX's collectives and lax.ppermute only.
A program may use at most 128 MiB of HBM per device.

```python
import jax
import jax.numpy as jnp
from jax import lax

H = 128
DL = 512
DK = 576
IH = 64
ID = 128
BLK = 64
TILE = 8
CTX_DEV = 128
SESS = 2
CTX = 1024
QTOK = 64
NBLK = 16
NSEL = 4
N_CTX = 8


def shared_rows(key):
    return jax.random.normal(key, (SESS, QTOK, DK), jnp.float32)


def session_lengths(key, part):
    lower = CTX // 2
    spread = CTX - BLK - lower + 1
    offset = jax.random.randint(key, (SESS,), 0, spread) + jnp.asarray(part).astype(jnp.int32)
    drawn = lower + offset % spread
    return jnp.where(jnp.arange(SESS) == 0, CTX, drawn).astype(jnp.int32)


def draw_kv_new(key, part):
    return shared_rows(key).astype(jnp.bfloat16)


def draw_q_latent(key, part):
    key = jax.random.fold_in(key, 11)
    noise = jax.random.normal(key, (SESS, QTOK, H, DK), jnp.float32)
    result = noise
    return result.astype(jnp.bfloat16)


def draw_context_len(key, part):
    return session_lengths(key, part)


def draw_block_list(key, part):
    lengths = session_lengths(key, part)
    key = jax.random.fold_in(key, 7)
    first_key, second_key = jax.random.split(key)
    blocks_dev = CTX_DEV // BLK
    owner_ids = jnp.arange(N_CTX, dtype=jnp.int32)
    valid_owners = (lengths + CTX_DEV - 1) // CTX_DEV
    raw_scores = jax.random.randint(first_key, (SESS, N_CTX, N_CTX), 0, 1 << 20) * N_CTX + owner_ids
    ranked = jnp.where(owner_ids[None, None, :] < valid_owners[:, None, None], raw_scores, -1 - owner_ids)
    unused, chosen = lax.top_k(ranked, NSEL)
    chosen = chosen.astype(jnp.int32)
    room = (lengths[:, None, None] - chosen * CTX_DEV + BLK - 1) // BLK
    room = jnp.clip(room, 1, blocks_dev)
    picked = jax.random.randint(second_key, (SESS, N_CTX, NSEL), 0, blocks_dev) % room
    return (chosen * blocks_dev + picked).astype(jnp.int32)


def shard_levels(stream_key, extent, shards, low, high):
    def one(axis_at, parts):
        steps = jax.random.uniform(jax.random.fold_in(jax.random.fold_in(stream_key, 6), axis_at), (parts,), jnp.float32, low / len(shards), high / len(shards))
        return jnp.repeat(jnp.exp(steps), extent[axis_at] // parts).reshape((-1,) + (1,) * (len(extent) - axis_at - 1))

    loudness = one(*shards[0])
    for cut in shards[1:]:
        loudness = loudness * one(*cut)
    return loudness


def scatter_about(stream_key, shape, width, bound, pieces=(), held_as=jnp.bfloat16):
    entries = jax.random.normal(stream_key, shape, jnp.float32) * width
    if len(pieces) > 0:
        entries = shard_levels(stream_key, shape, pieces, -0.22, 0.18) * entries
    return jnp.clip(entries, min=-bound, max=bound).astype(held_as)


def setup_inputs(seed: int = 0, part: int = 0) -> dict:
    key_of = jax.random.split(jax.random.key(seed), 9)
    part_keys = jax.random.split(jax.random.fold_in(key_of[8], part), 9)
    return {
        "q_latent": draw_q_latent(jax.random.fold_in(jax.random.fold_in(key_of[8], part), 71), part),
        "kv_new": draw_kv_new(jax.random.fold_in(jax.random.fold_in(key_of[8], part), 71), part),
        "kv_cache": scatter_about(part_keys[2], (SESS, CTX, DK), 1.0, 6.0, ((0, 2), (1, 8))),
        "index_q": scatter_about(part_keys[3], (SESS, QTOK, IH, ID), 0.0884, 0.59765625, ((0, 2), (1, 8))),
        "index_weight": scatter_about(part_keys[4], (SESS, QTOK, IH), 0.5, 3.0, ((0, 2), (1, 8))),
        "index_keys": scatter_about(part_keys[5], (SESS, CTX, ID), 1.0, 6.0, ((0, 2), (1, 8))),
        "block_list": draw_block_list(jax.random.fold_in(jax.random.fold_in(key_of[8], part), 71), part),
        "context_len": draw_context_len(jax.random.fold_in(jax.random.fold_in(key_of[8], part), 71), part),
    }


softmax_scale = 0.07216878364870322
neg_fill = -1.0e30


def tile_attention(query, new_rows, chosen, cache_blocks, length):
    cached_rows = cache_blocks[chosen].reshape(NSEL * BLK, DK)
    positions = (chosen[:, None] * BLK + jnp.arange(BLK)[None, :]).reshape(NSEL * BLK)
    key_rows = jnp.concatenate([cached_rows, new_rows], axis=0)
    query_rows = query.reshape(TILE * H, DK)
    scores = jnp.dot(query_rows, key_rows.T, preferred_element_type=jnp.float32) * softmax_scale
    cache_ok = positions < length
    token_of = jnp.arange(TILE * H) // H
    new_ok = jnp.arange(TILE)[None, :] <= token_of[:, None]
    allowed = jnp.concatenate([jnp.broadcast_to(cache_ok[None, :], (TILE * H, NSEL * BLK)), new_ok], axis=1)
    scores = jnp.where(allowed, scores, neg_fill)
    highest = jnp.max(scores, axis=1, keepdims=True)
    expo = jnp.exp(scores - highest)
    total = jnp.sum(expo, axis=1, keepdims=True)
    probs = expo.astype(jnp.bfloat16)
    mixed = jnp.dot(probs, key_rows[:, :DL], preferred_element_type=jnp.float32) / total
    return mixed.astype(jnp.bfloat16).reshape(TILE, H, DL)


def tile_index(index_rows, head_weight, key_table, length):
    products = jnp.dot(index_rows.reshape(TILE * IH, ID), key_table.T, preferred_element_type=jnp.float32)
    activ = jnp.maximum(products, 0.0).reshape(TILE, IH, CTX)
    weighted = jnp.einsum("tjr,tj->tr", activ, head_weight.astype(jnp.float32), precision=lax.Precision.HIGHEST)
    weighted = jnp.where(jnp.arange(CTX)[None, :] < length, weighted, 0.0)
    return weighted.reshape(TILE, NBLK, BLK).sum(axis=2) / BLK


def reference(q_latent, kv_new, kv_cache, index_q, index_weight, index_keys, block_list, context_len):
    attended_list = []
    score_list = []
    for session in range(SESS):
        cache_blocks = kv_cache[session].reshape(NBLK, BLK, DK)
        length = context_len[session]
        key_table = index_keys[session]

        def one_tile(tile_items):
            query, new_rows, index_rows, head_weight, chosen = tile_items
            return (tile_attention(query, new_rows, chosen, cache_blocks, length),
                    tile_index(index_rows, head_weight, key_table, length))

        attn_tiles, score_tiles = lax.map(one_tile, (
            q_latent[session].reshape(N_CTX, TILE, H, DK),
            kv_new[session].reshape(N_CTX, TILE, DK),
            index_q[session].reshape(N_CTX, TILE, IH, ID),
            index_weight[session].reshape(N_CTX, TILE, IH),
            block_list[session]))
        attended_list.append(attn_tiles.reshape(QTOK, H, DL))
        score_list.append(score_tiles.reshape(QTOK, NBLK))
    return jnp.stack(attended_list), jnp.stack(score_list)
```

```python
import functools
import math

import jax
import jax.numpy as jnp
from jax import lax
from jax.experimental import pallas as pl
from jax.experimental.pallas import tpu as pltpu
from jax.sharding import PartitionSpec as P

DR = 64
BLK = 64


softmax_scale = 0.07216878364870322
neg_fill = -1e30
F32 = jnp.float32
BF16 = jnp.bfloat16


def nt_dot(a, b):
    return lax.dot_general(a, b, (((1,), (1,)), ((), ())), preferred_element_type=F32)


def lanes_from(source_of_lane, on):
    row = lax.broadcasted_iota(jnp.int32, (2 * BLK, 2 * BLK), 0)
    return jnp.where((row == source_of_lane) & on, 1.0, 0.0).astype(BF16)


def prep_kernel(width, count, list_ref, pages_ref, keys_ref, out_ref):
    me = lax.axis_index("ctx")
    out_ref[0:width, :] = pages_ref[...]
    rows = keys_ref.shape[0]
    out_ref[width : width + rows, :] = keys_ref[...]
    row = lax.broadcasted_iota(jnp.int32, (16, 2 * BLK), 0)
    flags = jnp.zeros((16, 2 * BLK), F32)
    other = jnp.bitwise_xor(me, 1)
    for place, step in enumerate((count - 2, 2, 4)):
        holder = lax.rem(other + step, count)
        upper = jnp.int32(0)
        for j in range(list_ref.shape[0]):
            upper = jnp.where(list_ref[j] == 2 * holder + 1, 1, upper)
        flags = jnp.where(row == place, upper.astype(F32), flags)
    out_ref[width + rows :, :] = flags.astype(BF16)


def wanted_half(flag, lower_lanes):
    lane = lax.broadcasted_iota(jnp.int32, (2 * BLK, 2 * BLK), 1)
    upper = flag.astype(F32).astype(jnp.int32) * BLK
    if lower_lanes:
        return lanes_from(lane + upper, lane < BLK)
    return lanes_from(lane - BLK + upper, lane >= BLK)


def pick_two_kernel(width, flags_ref, before_ref, after_ref, out_ref):
    flags = flags_ref[...]
    both = jnp.dot(before_ref[0:width, :], wanted_half(flags[0:1, :], True), preferred_element_type=F32)
    both += jnp.dot(after_ref[0:width, :], wanted_half(flags[1:2, :], False), preferred_element_type=F32)
    out_ref[0:width, :] = both.astype(BF16)
    rows = 2 * BLK
    out_ref[width : width + rows, :] = before_ref[width : width + rows, :]
    out_ref[width + rows : width + 2 * rows, :] = after_ref[width : width + rows, :]


def pick_one_kernel(width, top, flags_ref, far_ref, out_ref):
    flag = flags_ref[2:3, :]
    low = width - top
    upper = jnp.dot(far_ref[top:width, :], wanted_half(flag, False), preferred_element_type=F32)
    lower = jnp.dot(far_ref[0:top, :], wanted_half(flag, True), preferred_element_type=F32)
    out_ref[0:top, :] = (upper[0:top, :] + lower).astype(BF16)
    out_ref[top:low, :] = upper[top:low, :].astype(BF16)
    rows = 2 * BLK
    out_ref[low : low + rows, :] = far_ref[width : width + rows, :]


def q_rows_kernel(q_ref, out_ref):
    tokens, _, heads = q_ref.shape
    for t in range(tokens):
        out_ref[t * heads : (t + 1) * heads, :] = q_ref[t].T


def index_kernel(
    count, width, low, length_ref, weight_ref, query_ref, own, near, below, above, far, two, one, out_ref, sums
):
    me = lax.axis_index("ctx")
    length = length_ref[0]
    rows = 2 * BLK
    query = query_ref[...]
    total = query.shape[0]
    row = lax.broadcasted_iota(jnp.int32, (rows, 1), 0)
    mate = jnp.bitwise_xor(me, 1)
    parts = (
        (own, width, me),
        (near, width, mate),
        (below, width, me + count - 2),
        (above, width, me + 2),
        (far, width, me + 4),
        (two, width, mate + count - 2),
        (two, width + rows, mate + 2),
        (one, low, mate + 4),
    )
    for ref, start, holder in parts:
        holder = lax.rem(holder, count)
        keys = ref[start : start + rows, :]
        keys = jnp.where(row < length - holder * rows, keys, jnp.zeros((), BF16))
        activ = jnp.maximum(nt_dot(keys, query), 0.0)
        sums[pl.ds(2 * holder, 1), :] = jnp.sum(activ[0:BLK, :], axis=0, keepdims=True)
        sums[pl.ds(2 * holder + 1, 1), :] = jnp.sum(activ[BLK:rows, :], axis=0, keepdims=True)
    weight = weight_ref[...].astype(F32)
    tokens, heads = weight.shape
    wide = jnp.concatenate([weight] * tokens, axis=1)
    lane = lax.broadcasted_iota(jnp.int32, (tokens, total), 1)
    token = lax.broadcasted_iota(jnp.int32, (tokens, total), 0)
    wide = jnp.where(lane // heads == token, wide, 0.0)
    score = lax.dot_general(
        wide, sums[...], (((1,), (1,)), ((), ())), precision=lax.Precision.HIGHEST, preferred_element_type=F32
    )
    out_ref[...] = score * (1.0 / BLK)


def attend_kernel(
    count, width, latent, top, list_ref, length_ref, q_ref, new_ref, own, near, below, above, far, two, one,
    out_ref, upper_rows, lower_rows, key_rows,
):
    me = lax.axis_index("ctx")
    length = length_ref[0]
    low = width - top
    for slot, ref in enumerate((own, above, far, below, near, two)):
        upper_rows[slot] = ref[0:top, :]
        lower_rows[slot] = ref[top:width, :]
    upper_rows[6] = one[0:top, :]
    lower_rows[6] = one[0:low, :]
    pages = list_ref.shape[0]
    tokens = new_ref.shape[0]
    key_rows[pages * BLK :, :] = jnp.zeros((key_rows.shape[0] - pages * BLK, width), BF16)
    key_rows[pages * BLK : pages * BLK + tokens, :] = new_ref[...]
    row = lax.broadcasted_iota(jnp.int32, (BLK, 2 * BLK), 0)
    lane = lax.broadcasted_iota(jnp.int32, (BLK, 2 * BLK), 1)
    wide = key_rows.shape[0]
    column = lax.broadcasted_iota(jnp.int32, (1, wide), 1)
    limit = jnp.zeros((1, wide), jnp.int32)
    for j in range(pages):
        page = list_ref[j]
        holder, half = page // 2, lax.rem(page, 2)
        step = lax.rem((holder // 2) - (me // 2) + count // 2, count // 2)
        same = lax.rem(holder + me, 2) == 0
        slot = jnp.where(same, step, jnp.where(step == 0, 4, jnp.where(step == 2, 6, 5)))
        high = jnp.where(same | (step == 0), half, jnp.where(step == 1, 1, 0))
        high_low = jnp.where(slot == 6, 1, high)
        pick_upper = jnp.where(lane == row + high * BLK, 1.0, 0.0).astype(BF16)
        pick_lower = jnp.where(lane == row + high_low * BLK, 1.0, 0.0).astype(BF16)
        place = slice(j * BLK, (j + 1) * BLK)
        key_rows[place, 0:top] = nt_dot(pick_upper, upper_rows[slot]).astype(BF16)
        key_rows[place, top:width] = nt_dot(pick_lower, lower_rows[slot]).astype(BF16)
        limit = jnp.where(column // BLK == j, length - page * BLK + j * BLK, limit)
    heads = q_ref.shape[0] // tokens
    keys = key_rows[...]
    values = key_rows[:, 0:latent]
    for t in range(tokens):
        bound = jnp.where(column >= pages * BLK, pages * BLK + t + 1, limit)
        place = slice(t * heads, (t + 1) * heads)
        scores = nt_dot(q_ref[place, :], keys) * softmax_scale
        scores = jnp.where(column < bound, scores, neg_fill)
        highest = jnp.max(scores, axis=1, keepdims=True)
        expo = jnp.exp(scores - highest)
        total = jnp.sum(expo, axis=1, keepdims=True)
        mixed = jnp.dot(expo.astype(BF16), values, preferred_element_type=F32) / total
        out_ref[place, :] = mixed.astype(BF16)


VMEM = pl.BlockSpec(memory_space=pltpu.VMEM)
SMEM = pl.BlockSpec(memory_space=pltpu.SMEM)


def call(body, shape, in_specs, scratch=(), flops=0, moved=0):
    return pl.pallas_call(
        body,
        out_shape=jax.ShapeDtypeStruct(*shape),
        in_specs=in_specs,
        out_specs=VMEM,
        scratch_shapes=scratch,
        cost_estimate=pl.CostEstimate(flops=flops, bytes_accessed=moved, transcendentals=0),
        compiler_params=pltpu.CompilerParams(vmem_limit_bytes=32 * 1024 * 1024),
    )


def on_ring(
    q_latent, kv_new, kv_cache, index_q, index_weight, index_keys, block_list, context_len
):
    count = lax.axis_size("ctx")
    tile_len, head_count, width = q_latent.shape[1:]
    latent = width - DR
    rows = kv_cache.shape[1]
    chosen = block_list[0, 0]
    top = 256
    low = width - top
    pages = kv_cache[0].T
    query = jnp.transpose(q_latent[0], (0, 2, 1))

    def shift(x, by):
        return lax.ppermute(x, "ctx", [(i, (i + by) % count) for i in range(count)])

    def swap(x):
        return lax.ppermute(x, "ctx", [(i, i ^ 1) for i in range(count)])

    whole = width + rows + 16
    own = call(
        functools.partial(prep_kernel, width, count), ((whole, rows), BF16), [SMEM, VMEM, VMEM], moved=2 * whole * rows * 2
    )(chosen, pages, index_keys[0])
    near = swap(own)
    below = shift(own, 2)
    above = shift(own, -2)
    far = shift(own, 4)
    flags = near[width + rows :, :]
    two = swap(
        call(functools.partial(pick_two_kernel, width), ((width + 2 * rows, rows), BF16), [VMEM] * 3)(flags, below, above)
    )
    one = swap(
        call(functools.partial(pick_one_kernel, width, top), ((low + rows, rows), BF16), [VMEM] * 2)(flags, far)
    )
    q_rows = call(q_rows_kernel, ((tile_len * head_count, width), BF16), [VMEM], moved=4 * tile_len * head_count * width)(query)
    index_rows = index_q[0].reshape(-1, index_q.shape[3])
    block_score = call(
        functools.partial(index_kernel, count, width, low),
        ((tile_len, 2 * count), F32),
        [SMEM] + [VMEM] * 9,
        [pltpu.VMEM((2 * count, index_rows.shape[0]), F32)],
    )(context_len, index_weight[0], index_rows, own, near, below, above, far, two, one)
    wide = -(-(chosen.shape[0] * BLK + tile_len) // 128) * 128
    attended = call(
        functools.partial(attend_kernel, count, width, latent, top),
        ((tile_len * head_count, latent), BF16),
        [SMEM] * 2 + [VMEM] * 9,
        [pltpu.VMEM((7, top, rows), BF16), pltpu.VMEM((7, low, rows), BF16), pltpu.VMEM((wide, width), BF16)],
    )(chosen, context_len, q_rows, kv_new[0], own, near, below, above, far, two, one)
    return attended.reshape(1, tile_len, head_count, latent), block_score[None]


def on_device(
    q_latent, kv_new, kv_cache, index_q, index_weight, index_keys, block_list, context_len
):
    ctx_count = lax.axis_size("ctx")
    my_index = lax.axis_index("ctx")
    tile_len = q_latent.shape[1]
    head_count = q_latent.shape[2]
    row_width = q_latent.shape[3]
    latent_width = row_width - DR
    ctx_rows = kv_cache.shape[1]
    blocks_dev = ctx_rows // BLK
    block_total = blocks_dev * ctx_count
    index_heads = index_q.shape[2]
    index_width = index_q.shape[3]
    length = context_len[0]
    head_weight = index_weight[0]
    index_rows = index_q[0].reshape(tile_len * index_heads, index_width)
    weight_f32 = head_weight.astype(jnp.float32)
    piece = lax.all_gather(index_keys[0], "ctx", axis=0, tiled=True)
    count = piece.shape[0]
    products = jnp.dot(index_rows, piece.T, preferred_element_type=jnp.float32)
    activ = jnp.maximum(products, 0.0).reshape(tile_len, index_heads, count)
    weighted = jnp.einsum("tjr,tj->tr", activ, weight_f32, precision=lax.Precision.HIGHEST)
    positions = jnp.arange(count)
    weighted = jnp.where(positions[None, :] < length, weighted, 0.0)
    summed = jax.ops.segment_sum(weighted.T, positions // BLK, num_segments=block_total)
    block_sums = summed.T
    block_score = (block_sums / BLK).reshape(1, tile_len, block_total)
    all_lists = lax.all_gather(block_list[0], "ctx", axis=0, tiled=True)
    is_mine = all_lists // blocks_dev == my_index
    slot_index = jnp.sum(jnp.where(is_mine, all_lists % blocks_dev, 0), axis=1)
    wanted = jnp.any(is_mine, axis=1)
    own_blocks = kv_cache[0].reshape(blocks_dev, BLK, row_width)
    outgoing = jnp.where(wanted[:, None, None], own_blocks[slot_index], jnp.zeros((), jnp.bfloat16))
    incoming = lax.all_to_all(outgoing, "ctx", split_axis=0, concat_axis=0, tiled=True)
    chosen = block_list[0, 0]
    cached_rows = incoming[chosen // blocks_dev].reshape(-1, row_width)
    positions = (chosen[:, None] * BLK + jnp.arange(BLK)[None, :]).reshape(-1)
    key_rows = jnp.concatenate([cached_rows, kv_new[0]], axis=0)
    query_rows = q_latent[0].reshape(tile_len * head_count, row_width)
    scores = jnp.dot(query_rows, key_rows.T, preferred_element_type=jnp.float32) * softmax_scale
    cache_ok = positions < length
    token_of = jnp.arange(tile_len * head_count) // head_count
    new_ok = jnp.arange(tile_len)[None, :] <= token_of[:, None]
    allowed = jnp.concatenate(
        [
            jnp.broadcast_to(cache_ok[None, :], (tile_len * head_count, cached_rows.shape[0])),
            new_ok,
        ],
        axis=1,
    )
    scores = jnp.where(allowed, scores, neg_fill)
    highest = jnp.max(scores, axis=1, keepdims=True)
    expo = jnp.exp(scores - highest)
    total = jnp.sum(expo, axis=1, keepdims=True)
    probs = expo.astype(jnp.bfloat16)
    mixed = jnp.dot(probs, key_rows[:, :latent_width], preferred_element_type=jnp.float32) / total
    attended = mixed.astype(jnp.bfloat16).reshape(1, tile_len, head_count, latent_width)
    return (attended, block_score)


def solution(mesh):
    placed = (
        P(("groups", "batch"), "ctx", None, None),
        P(("groups", "batch"), "ctx", None),
        P(("groups", "batch"), "ctx", None),
        P(("groups", "batch"), "ctx", None, None),
        P(("groups", "batch"), "ctx", None),
        P(("groups", "batch"), "ctx", None),
        P(("groups", "batch"), "ctx", None),
        P(("groups", "batch")),
    )
    return jax.shard_map(
        on_ring if mesh.shape["ctx"] == 8 else on_device,
        mesh=mesh,
        in_specs=placed,
        out_specs=(P(("groups", "batch"), "ctx", None, None), P(("groups", "batch"), "ctx", None)),
        check_vma=False,
    )
```

```python
import functools
import math

import jax
import jax.numpy as jnp
from jax import lax
from jax.experimental import pallas as pl
from jax.experimental.pallas import tpu as pltpu
from jax.sharding import PartitionSpec as P

DR = 64
BLK = 64


softmax_scale = 0.07216878364870322
neg_fill = -1e30
F32 = jnp.float32
BF16 = jnp.bfloat16


def nt_dot(a, b):
    return lax.dot_general(a, b, (((1,), (1,)), ((), ())), preferred_element_type=F32)


def turn(x):
    return jnp.concatenate([x[:, BLK:], x[:, :BLK]], axis=1)


def pick_kernel(step, count, width, top, list_ref, line_ref, out_ref):
    holder = lax.rem(lax.axis_index("ctx") + step, count)
    asked = jnp.where(list_ref[...] == 2 * holder + 1, 1.0, 0.0)
    upper = jnp.max(asked, axis=1, keepdims=True) > 0.5
    low = width - top
    rows = 2 * BLK
    lane = lax.broadcasted_iota(jnp.int32, (1, rows), 1)
    keep = jnp.logical_xor(lane < BLK, upper)
    first = line_ref[0:low, :].astype(F32)
    second = line_ref[top:width, :].astype(F32)
    first = jnp.where(upper, turn(first), first)
    second = jnp.where(upper, second, turn(second))
    out_ref[0:low, :] = jnp.where(lane < BLK, first, second).astype(BF16)
    out_ref[low : low + rows, :] = line_ref[width : width + rows, :]


def prepare_kernel(q_hbm, new_hbm, rows_ref, scores_ref, new_rows_ref, q_ref, new_ref, sems):
    tokens, _, heads = q_ref.shape
    first = pltpu.make_async_copy(new_hbm, new_ref.at[0:tokens], sems.at[tokens])
    first.start()
    copies = [pltpu.make_async_copy(q_hbm.at[t], q_ref.at[t], sems.at[t]) for t in range(tokens)]
    for copy in copies:
        copy.start()
    new_ref[tokens:, :] = jnp.zeros_like(new_ref[tokens:, :])
    first.wait()
    new_rows_ref[...] = new_ref[:, 0 : new_rows_ref.shape[1]]
    column = lax.broadcasted_iota(jnp.int32, (1, new_ref.shape[0]), 1)
    for t in range(tokens):
        copies[t].wait()
        rows_ref[t * heads : (t + 1) * heads, :] = q_ref[t].T
    scores = nt_dot(rows_ref[...], new_ref[...])
    for t in range(tokens):
        place = slice(t * heads, (t + 1) * heads)
        scores_ref[place, :] = jnp.where(column <= t, scores[place, :], neg_fill)


def page_sums(keys, query, room, holder, sums):
    rows = 2 * BLK
    row = lax.broadcasted_iota(jnp.int32, (rows, rows), 0)
    keys = jnp.where(row < room, keys, jnp.zeros((), BF16))
    activ = jnp.maximum(nt_dot(keys, query), 0.0)
    sums[pl.ds(2 * holder, 1), :] = jnp.sum(activ[0:BLK, :], axis=0, keepdims=True)
    sums[pl.ds(2 * holder + 1, 1), :] = jnp.sum(activ[BLK:rows, :], axis=0, keepdims=True)


def weigh(weight_ref, sums):
    weight = weight_ref[...].astype(F32)
    tokens, heads = weight.shape
    total = sums.shape[1]
    lane = lax.broadcasted_iota(jnp.int32, (tokens, total), 1)
    token = lax.broadcasted_iota(jnp.int32, (tokens, total), 0)
    wide = jnp.where(lane // heads == token, jnp.concatenate([weight] * tokens, axis=1), 0.0)
    score = lax.dot_general(
        wide, sums[...], (((1,), (1,)), ((), ())), precision=lax.Precision.HIGHEST, preferred_element_type=F32
    )
    return score * (1.0 / BLK)


def early_kernel(
    count, width, latent, top, list_ref, length_ref, weight_ref, query_ref,
    own, near, below, above, far, side_below, side_above,
    score_ref, turned_ref, rows_ref, marks_ref, slots, sums,
):
    me = lax.axis_index("ctx")
    mate = jnp.bitwise_xor(me, 1)
    last = lax.rem(mate + 4, count)
    low = width - top
    rows = 2 * BLK
    for slot, ref in enumerate((own, above, far, below, near)):
        slots[slot] = ref[0:width, :]
    for slot, ref in ((5, side_above), (7, side_below)):
        slots[slot, 0:top, :] = ref[0:top, :]
        slots[slot, top:width, :] = turn(ref[0:low, :].astype(F32)).astype(BF16)
    slots[6] = jnp.zeros((width, rows), BF16)
    lane = lax.broadcasted_iota(jnp.int32, (1, rows), 1)
    column = lax.broadcasted_iota(jnp.int32, (1, list_ref.shape[0] * BLK), 1)
    limit = jnp.zeros_like(column)
    late = jnp.zeros_like(column)
    length = length_ref[0]
    pages = list_ref.shape[0]
    for pair in range(pages // 2):
        halves = []
        for j in (2 * pair, 2 * pair + 1):
            page = list_ref[j]
            holder, half = page // 2, lax.rem(page, 2)
            step = lax.rem((holder // 2) - (me // 2) + count // 2, count // 2)
            same = lax.rem(holder + me, 2) == 0
            slot = jnp.where(same, step, 4 + step)
            high = jnp.where(same | (step == 0), half, 0)
            block = slots[slot].astype(F32)
            halves.append(jnp.where(high == j - 2 * pair, block, turn(block)))
            limit = jnp.where(column // BLK == j, length - page * BLK + j * BLK, limit)
            late = jnp.where((column // BLK == j) & (holder == last), 1, late)
        block = jnp.where(lane < BLK, halves[0], halves[1]).astype(BF16)
        place = slice(pair * rows, (pair + 1) * rows)
        turned_ref[:, place] = block
        rows_ref[place, :] = block[0:latent, :].T
    marks_ref[0:1, :] = limit
    marks_ref[1:2, :] = late
    marks_ref[2:3, :] = jnp.full_like(column, length - last * rows)
    query = query_ref[...]
    sums[pl.ds(2 * last, 1), :] = jnp.zeros((1, sums.shape[1]), F32)
    sums[pl.ds(2 * last + 1, 1), :] = jnp.zeros((1, sums.shape[1]), F32)
    for ref, start, holder in (
        (own, width, me),
        (near, width, mate),
        (below, width, me + count - 2),
        (above, width, me + 2),
        (far, width, me + 4),
        (side_below, low, mate + count - 2),
        (side_above, low, mate + 2),
    ):
        holder = lax.rem(holder, count)
        page_sums(ref[start : start + rows, :], query, length - holder * rows, holder, sums)
    score_ref[...] = weigh(weight_ref, sums)


def attend_kernel(
    count, width, latent, top, chunk, q_ref, fresh_ref, new_rows, early_turned, early_rows, marks_ref, early_score, side_far, weight_ref, query_ref,
    out_hbm, score_hbm, turned, key_rows, sums, out_ref, score_ref, sems,
):
    me = lax.axis_index("ctx")
    last = lax.rem(jnp.bitwise_xor(me, 1) + 4, count)
    low = width - top
    rows = 2 * BLK
    sums[...] = jnp.zeros_like(sums)
    page_sums(side_far[low : low + rows, :], query_ref[...], marks_ref[2:3, 0:rows], last, sums)
    score_ref[...] = early_score[...] + weigh(weight_ref, sums)
    steps = q_ref.shape[0] // chunk
    copies = [pltpu.make_async_copy(score_ref, score_hbm, sems.at[steps])]
    copies[0].start()
    lane = lax.broadcasted_iota(jnp.int32, (1, rows), 1)
    packed = side_far[0:low, :].astype(F32)
    swapped = turn(packed)
    first = jnp.concatenate([packed[0:top], swapped], axis=0)
    second = jnp.concatenate([swapped[0:top], packed], axis=0)
    both = jnp.where(lane < BLK, first, second).astype(BF16)
    both_rows = both[0:latent, :].T
    limit = marks_ref[0:1, :]
    late = marks_ref[1:2, :]
    for place in range(0, turned.shape[1], rows):
        place = slice(place, place + rows)
        turned[:, place] = jnp.where(late[:, place] == 1, both, early_turned[:, place])
        down = jnp.broadcast_to(late[:, place].astype(F32), (rows, rows)).T[:, 0:1]
        key_rows[place, :] = jnp.where(down > 0.5, both_rows, early_rows[place, :])
    factor = softmax_scale * math.log2(math.e)
    column = lax.broadcasted_iota(jnp.int32, (1, turned.shape[1]), 1)
    for step in range(steps):
        place = slice(step * chunk, (step + 1) * chunk)
        scores = jnp.dot(q_ref[place, :], turned[...], preferred_element_type=F32)
        scores = jnp.where(column < limit, scores, neg_fill)
        fresh = fresh_ref[place, :]
        highest = jnp.maximum(jnp.max(scores, axis=1, keepdims=True), jnp.max(fresh, axis=1, keepdims=True))
        expo = jnp.exp2((scores - highest) * factor)
        expo_new = jnp.exp2((fresh - highest) * factor)
        total = jnp.sum(expo, axis=1, keepdims=True) + jnp.sum(expo_new, axis=1, keepdims=True)
        probs = jnp.concatenate([expo.astype(BF16), expo_new.astype(BF16)], axis=1)
        values = jnp.concatenate([key_rows[...], new_rows[...]], axis=0)
        mixed = jnp.dot(probs, values, preferred_element_type=F32)
        out_ref[place, :] = (mixed / total).astype(BF16)
        copies.append(pltpu.make_async_copy(out_ref.at[place], out_hbm.at[place], sems.at[step]))
        copies[-1].start()
    for copy in copies:
        copy.wait()


VMEM = pl.BlockSpec(memory_space=pltpu.VMEM)
SMEM = pl.BlockSpec(memory_space=pltpu.SMEM)


ANY = pl.BlockSpec(memory_space=pl.ANY)


def call(body, shapes, in_specs, out_specs=VMEM, scratch=(), flops=0, moved=0, vmem=32):
    return pl.pallas_call(
        body,
        out_shape=shapes,
        in_specs=in_specs,
        out_specs=out_specs,
        scratch_shapes=scratch,
        cost_estimate=pl.CostEstimate(flops=flops, bytes_accessed=moved, transcendentals=0),
        compiler_params=pltpu.CompilerParams(vmem_limit_bytes=vmem * 1024 * 1024),
    )


def on_ring(
    q_latent, kv_new, kv_cache, index_q, index_weight, index_keys, block_list, context_len
):
    count = lax.axis_size("ctx")
    tile_len, head_count, width = q_latent.shape[1:]
    latent = width - DR
    rows = kv_cache.shape[1]
    chosen = block_list[0, 0]
    top = 256
    low = width - top
    pages = kv_cache[0].T
    query = jnp.transpose(q_latent[0], (0, 2, 1))
    shape = jax.ShapeDtypeStruct

    def shift(x, by):
        return lax.ppermute(x, "ctx", [(i, (i + by) % count) for i in range(count)])

    def swap(x):
        return lax.ppermute(x, "ctx", [(i, i ^ 1) for i in range(count)])

    def pick(step, line):
        body = functools.partial(pick_kernel, step, count, width, top)
        return call(body, shape((low + rows, rows), BF16), [VMEM] * 2, moved=2 * 10**6)(asked, line)

    own = jnp.concatenate([pages, index_keys[0]], axis=0)
    below = shift(own, 2)
    near = swap(own)
    above = shift(own, -2)
    asked = swap(block_list[0])
    query_count = tile_len * head_count
    index_rows = index_q[0].reshape(-1, index_q.shape[3])
    q_rows, fresh, new_rows = call(
        prepare_kernel,
        (shape((query_count, width), BF16), shape((query_count, 128), F32), shape((128, latent), BF16)),
        [ANY] * 2,
        (VMEM,) * 3,
        [
            pltpu.VMEM(query.shape, BF16),
            pltpu.VMEM((128, width), BF16),
            pltpu.SemaphoreType.DMA((tile_len + 1,)),
        ],
        moved=4 * query_count * width,
        vmem=56,
    )(query, kv_new[0])
    below, asked = lax.optimization_barrier((below, asked))
    far = shift(below, 2)
    asked, near, q_rows, fresh = lax.optimization_barrier((asked, near, q_rows, fresh))
    side_below = swap(pick(count - 2, below))
    side_above = swap(pick(2, above))
    side_far = swap(pick(4, far))
    sums = pltpu.VMEM((2 * count, index_rows.shape[0]), F32)
    columns = chosen.shape[0] * BLK
    score, turned, key_rows, marks = call(
        functools.partial(early_kernel, count, width, latent, top),
        (shape((tile_len, 2 * count), F32), shape((width, columns), BF16), shape((columns, latent), BF16), shape((8, columns), jnp.int32)),
        [SMEM] * 2 + [VMEM] * 9,
        (VMEM,) * 4,
        [pltpu.VMEM((8, width, rows), BF16), sums],
        moved=4 * query_count * width,
    )(chosen, context_len, index_weight[0], index_rows, own, near, below, above, far, side_below, side_above)
    chunk = query_count // 2
    attended, block_score = call(
        functools.partial(attend_kernel, count, width, latent, top, chunk),
        (shape((query_count, latent), BF16), shape((tile_len, 2 * count), F32)),
        [VMEM] * 10,
        (ANY, ANY),
        [
            pltpu.VMEM((width, columns), BF16),
            pltpu.VMEM((columns, latent), BF16),
            sums,
            pltpu.VMEM((query_count, latent), BF16),
            pltpu.VMEM((tile_len, 2 * count), F32),
            pltpu.SemaphoreType.DMA((2 + 1,)),
        ],
    )(q_rows, fresh, new_rows, turned, key_rows, marks, score, side_far, index_weight[0], index_rows)
    return attended.reshape(1, tile_len, head_count, latent), block_score[None]


def on_device(
    q_latent, kv_new, kv_cache, index_q, index_weight, index_keys, block_list, context_len
):
    ctx_count = lax.axis_size("ctx")
    my_index = lax.axis_index("ctx")
    tile_len = q_latent.shape[1]
    head_count = q_latent.shape[2]
    row_width = q_latent.shape[3]
    latent_width = row_width - DR
    ctx_rows = kv_cache.shape[1]
    blocks_dev = ctx_rows // BLK
    block_total = blocks_dev * ctx_count
    index_heads = index_q.shape[2]
    index_width = index_q.shape[3]
    length = context_len[0]
    head_weight = index_weight[0]
    index_rows = index_q[0].reshape(tile_len * index_heads, index_width)
    weight_f32 = head_weight.astype(jnp.float32)
    piece = lax.all_gather(index_keys[0], "ctx", axis=0, tiled=True)
    count = piece.shape[0]
    products = jnp.dot(index_rows, piece.T, preferred_element_type=jnp.float32)
    activ = jnp.maximum(products, 0.0).reshape(tile_len, index_heads, count)
    weighted = jnp.einsum("tjr,tj->tr", activ, weight_f32, precision=lax.Precision.HIGHEST)
    positions = jnp.arange(count)
    weighted = jnp.where(positions[None, :] < length, weighted, 0.0)
    summed = jax.ops.segment_sum(weighted.T, positions // BLK, num_segments=block_total)
    block_sums = summed.T
    block_score = (block_sums / BLK).reshape(1, tile_len, block_total)
    all_lists = lax.all_gather(block_list[0], "ctx", axis=0, tiled=True)
    is_mine = all_lists // blocks_dev == my_index
    slot_index = jnp.sum(jnp.where(is_mine, all_lists % blocks_dev, 0), axis=1)
    wanted = jnp.any(is_mine, axis=1)
    own_blocks = kv_cache[0].reshape(blocks_dev, BLK, row_width)
    outgoing = jnp.where(wanted[:, None, None], own_blocks[slot_index], jnp.zeros((), jnp.bfloat16))
    incoming = lax.all_to_all(outgoing, "ctx", split_axis=0, concat_axis=0, tiled=True)
    chosen = block_list[0, 0]
    cached_rows = incoming[chosen // blocks_dev].reshape(-1, row_width)
    positions = (chosen[:, None] * BLK + jnp.arange(BLK)[None, :]).reshape(-1)
    key_rows = jnp.concatenate([cached_rows, kv_new[0]], axis=0)
    query_rows = q_latent[0].reshape(tile_len * head_count, row_width)
    scores = jnp.dot(query_rows, key_rows.T, preferred_element_type=jnp.float32) * softmax_scale
    cache_ok = positions < length
    token_of = jnp.arange(tile_len * head_count) // head_count
    new_ok = jnp.arange(tile_len)[None, :] <= token_of[:, None]
    allowed = jnp.concatenate(
        [
            jnp.broadcast_to(cache_ok[None, :], (tile_len * head_count, cached_rows.shape[0])),
            new_ok,
        ],
        axis=1,
    )
    scores = jnp.where(allowed, scores, neg_fill)
    highest = jnp.max(scores, axis=1, keepdims=True)
    expo = jnp.exp(scores - highest)
    total = jnp.sum(expo, axis=1, keepdims=True)
    probs = expo.astype(jnp.bfloat16)
    mixed = jnp.dot(probs, key_rows[:, :latent_width], preferred_element_type=jnp.float32) / total
    attended = mixed.astype(jnp.bfloat16).reshape(1, tile_len, head_count, latent_width)
    return (attended, block_score)


def solution(mesh):
    placed = (
        P(("groups", "batch"), "ctx", None, None),
        P(("groups", "batch"), "ctx", None),
        P(("groups", "batch"), "ctx", None),
        P(("groups", "batch"), "ctx", None, None),
        P(("groups", "batch"), "ctx", None),
        P(("groups", "batch"), "ctx", None),
        P(("groups", "batch"), "ctx", None),
        P(("groups", "batch")),
    )
    return jax.shard_map(
        on_ring if mesh.shape["ctx"] == 8 else on_device,
        mesh=mesh,
        in_specs=placed,
        out_specs=(P(("groups", "batch"), "ctx", None, None), P(("groups", "batch"), "ctx", None)),
        check_vma=False,
    )
```

```python
import functools
import math

import jax
import jax.numpy as jnp
from jax import lax
from jax.experimental import pallas as pl
from jax.experimental.pallas import tpu as pltpu
from jax.sharding import PartitionSpec as P

DR = 64
BLK = 64


softmax_scale = 0.07216878364870322
neg_fill = -1e30
F32 = jnp.float32
BF16 = jnp.bfloat16


def nt_dot(a, b):
    return lax.dot_general(a, b, (((1,), (1,)), ((), ())), preferred_element_type=F32)


def turn(x):
    return jnp.concatenate([x[:, BLK:], x[:, :BLK]], axis=1)


RING = (0, 2, 3, 1)


def ring_steps(me):
    level = me // 2
    odd = jnp.bitwise_xor(level, level // 2) % 2 != lax.axis_index("batch")
    return jnp.where(odd, 4, 2), jnp.where(odd, 2, 4), 6


def pick_kernel(step, width, top, list_ref, line_ref, out_ref):
    me = lax.axis_index("ctx")
    holder = jnp.bitwise_xor(me, ring_steps(me)[step])
    asked = jnp.where(list_ref[...] == 2 * holder + 1, 1.0, 0.0)
    upper = jnp.max(asked, axis=1, keepdims=True) > 0.5
    low = width - top
    rows = 2 * BLK
    lane = lax.broadcasted_iota(jnp.int32, (1, rows), 1)
    keep = jnp.logical_xor(lane < BLK, upper)
    first = line_ref[0:low, :].astype(F32)
    second = line_ref[top:width, :].astype(F32)
    first = jnp.where(upper, turn(first), first)
    second = jnp.where(upper, second, turn(second))
    out_ref[0:low, :] = jnp.where(lane < BLK, first, second).astype(BF16)
    out_ref[low : low + rows, :] = line_ref[width : width + rows, :]


def prepare_kernel(q_ref, new_ref, rows_ref, scores_ref, new_rows_ref, wide_ref):
    tokens, _, heads = q_ref.shape
    wide_ref[...] = jnp.zeros_like(wide_ref)
    wide_ref[0:tokens, :] = new_ref[...]
    new_rows_ref[...] = wide_ref[:, 0 : new_rows_ref.shape[1]]
    column = lax.broadcasted_iota(jnp.int32, (1, wide_ref.shape[0]), 1)
    for t in range(tokens):
        rows_ref[t * heads : (t + 1) * heads, :] = q_ref[t].T
    scores = nt_dot(rows_ref[...], wide_ref[...])
    for t in range(tokens):
        place = slice(t * heads, (t + 1) * heads)
        scores_ref[place, :] = jnp.where(column <= t, scores[place, :], neg_fill)


def page_sums(keys, query, room, holder, sums):
    rows = 2 * BLK
    row = lax.broadcasted_iota(jnp.int32, (rows, rows), 0)
    keys = jnp.where(row < room, keys, jnp.zeros((), BF16))
    activ = jnp.maximum(nt_dot(keys, query), 0.0)
    sums[pl.ds(2 * holder, 1), :] = jnp.sum(activ[0:BLK, :], axis=0, keepdims=True)
    sums[pl.ds(2 * holder + 1, 1), :] = jnp.sum(activ[BLK:rows, :], axis=0, keepdims=True)


def weigh(weight_ref, sums):
    weight = weight_ref[...].astype(F32)
    tokens, heads = weight.shape
    total = sums.shape[1]
    lane = lax.broadcasted_iota(jnp.int32, (tokens, total), 1)
    token = lax.broadcasted_iota(jnp.int32, (tokens, total), 0)
    wide = jnp.where(lane // heads == token, jnp.concatenate([weight] * tokens, axis=1), 0.0)
    score = lax.dot_general(
        wide, sums[...], (((1,), (1,)), ((), ())), precision=lax.Precision.HIGHEST, preferred_element_type=F32
    )
    return score * (1.0 / BLK)


def early_kernel(
    width, latent, top, list_ref, length_ref, weight_ref, query_ref,
    own, near, below, above, far, side_below, side_above,
    score_ref, turned_ref, rows_ref, marks_ref, slots, sums,
):
    me = lax.axis_index("ctx")
    behind, ahead, opposite = ring_steps(me)
    last = jnp.bitwise_xor(me, opposite + 1)
    low = width - top
    rows = 2 * BLK
    lane = lax.broadcasted_iota(jnp.int32, (1, rows), 1)
    for slot, ref in ((0, own), (1, near), (behind, below), (ahead, above), (opposite, far)):
        slots[slot] = ref[0:width, :]
    for slot, ref in ((behind + 1, side_below), (ahead + 1, side_above)):
        slots[slot, 0:top, :] = ref[0:top, :]
        slots[slot, top:width, :] = turn(ref[0:low, :].astype(F32)).astype(BF16)
    slots[opposite + 1] = jnp.zeros((width, rows), BF16)
    column = lax.broadcasted_iota(jnp.int32, (1, list_ref.shape[0] * BLK), 1)
    limit = jnp.zeros_like(column)
    late = jnp.zeros_like(column)
    length = length_ref[0]
    pages = list_ref.shape[0]
    for pair in range(pages // 2):
        halves = []
        for j in (2 * pair, 2 * pair + 1):
            page = list_ref[j]
            holder, half = page // 2, lax.rem(page, 2)
            slot = jnp.bitwise_xor(holder, me)
            high = jnp.where((slot == 1) | (lax.rem(slot, 2) == 0), half, 0)
            block = slots[slot].astype(F32)
            halves.append(jnp.where(high == j - 2 * pair, block, turn(block)))
            limit = jnp.where(column // BLK == j, length - page * BLK + j * BLK, limit)
            late = jnp.where((column // BLK == j) & (holder == last), 1, late)
        block = jnp.where(lane < BLK, halves[0], halves[1]).astype(BF16)
        place = slice(pair * rows, (pair + 1) * rows)
        turned_ref[:, place] = block
        rows_ref[place, :] = block[0:latent, :].T
    marks_ref[0:1, :] = limit
    marks_ref[1:2, :] = late
    marks_ref[2:3, :] = jnp.full_like(column, length - last * rows)
    query = query_ref[...]
    sums[pl.ds(2 * last, 1), :] = jnp.zeros((1, sums.shape[1]), F32)
    sums[pl.ds(2 * last + 1, 1), :] = jnp.zeros((1, sums.shape[1]), F32)
    for ref, start, step in (
        (own, width, 0),
        (near, width, 1),
        (below, width, behind),
        (above, width, ahead),
        (far, width, opposite),
        (side_below, low, behind + 1),
        (side_above, low, ahead + 1),
    ):
        holder = jnp.bitwise_xor(me, step)
        page_sums(ref[start : start + rows, :], query, length - holder * rows, holder, sums)
    score_ref[...] = weigh(weight_ref, sums)


def attend_kernel(
    width, latent, top, chunk, q_ref, fresh_ref, new_rows, early_turned, early_rows, marks_ref, early_score, side_far, weight_ref, query_ref,
    out_hbm, score_hbm, turned, key_rows, sums, out_ref, score_ref, sems,
):
    me = lax.axis_index("ctx")
    last = jnp.bitwise_xor(me, 7)
    low = width - top
    rows = 2 * BLK
    sums[...] = jnp.zeros_like(sums)
    page_sums(side_far[low : low + rows, :], query_ref[...], marks_ref[2:3, 0:rows], last, sums)
    score_ref[...] = early_score[...] + weigh(weight_ref, sums)
    steps = q_ref.shape[0] // chunk
    copies = [pltpu.make_async_copy(score_ref, score_hbm, sems.at[steps])]
    copies[0].start()
    lane = lax.broadcasted_iota(jnp.int32, (1, rows), 1)
    packed = side_far[0:low, :].astype(F32)
    swapped = turn(packed)
    first = jnp.concatenate([packed[0:top], swapped], axis=0)
    second = jnp.concatenate([swapped[0:top], packed], axis=0)
    both = jnp.where(lane < BLK, first, second).astype(BF16)
    both_rows = both[0:latent, :].T
    limit = marks_ref[0:1, :]
    late = marks_ref[1:2, :]
    for place in range(0, turned.shape[1], rows):
        place = slice(place, place + rows)
        turned[:, place] = jnp.where(late[:, place] == 1, both, early_turned[:, place])
        down = jnp.broadcast_to(late[:, place].astype(F32), (rows, rows)).T[:, 0:1]
        key_rows[place, :] = jnp.where(down > 0.5, both_rows, early_rows[place, :])
    factor = softmax_scale * math.log2(math.e)
    column = lax.broadcasted_iota(jnp.int32, (1, turned.shape[1]), 1)
    for step in range(steps):
        place = slice(step * chunk, (step + 1) * chunk)
        scores = jnp.dot(q_ref[place, :], turned[...], preferred_element_type=F32)
        scores = jnp.where(column < limit, scores, neg_fill)
        fresh = fresh_ref[place, :]
        highest = jnp.maximum(jnp.max(scores, axis=1, keepdims=True), jnp.max(fresh, axis=1, keepdims=True))
        expo = jnp.exp2((scores - highest) * factor)
        expo_new = jnp.exp2((fresh - highest) * factor)
        total = jnp.sum(expo, axis=1, keepdims=True) + jnp.sum(expo_new, axis=1, keepdims=True)
        probs = jnp.concatenate([expo.astype(BF16), expo_new.astype(BF16)], axis=1)
        values = jnp.concatenate([key_rows[...], new_rows[...]], axis=0)
        mixed = jnp.dot(probs, values, preferred_element_type=F32)
        out_ref[place, :] = (mixed / total).astype(BF16)
        copies.append(pltpu.make_async_copy(out_ref.at[place], out_hbm.at[place], sems.at[step]))
        copies[-1].start()
    for copy in copies:
        copy.wait()


VMEM = pl.BlockSpec(memory_space=pltpu.VMEM)
SMEM = pl.BlockSpec(memory_space=pltpu.SMEM)


ANY = pl.BlockSpec(memory_space=pl.ANY)


def call(body, shapes, in_specs, out_specs=VMEM, scratch=(), flops=0, moved=0, vmem=32):
    return pl.pallas_call(
        body,
        out_shape=shapes,
        in_specs=in_specs,
        out_specs=out_specs,
        scratch_shapes=scratch,
        cost_estimate=pl.CostEstimate(flops=flops, bytes_accessed=moved, transcendentals=0),
        compiler_params=pltpu.CompilerParams(vmem_limit_bytes=vmem * 1024 * 1024),
    )


def on_ring(
    q_latent, kv_new, kv_cache, index_q, index_weight, index_keys, block_list, context_len
):
    count = lax.axis_size("ctx")
    tile_len, head_count, width = q_latent.shape[1:]
    latent = width - DR
    rows = kv_cache.shape[1]
    chosen = block_list[0, 0]
    top = 256
    low = width - top
    pages = kv_cache[0].T
    query = jnp.transpose(q_latent[0], (0, 2, 1))
    shape = jax.ShapeDtypeStruct

    def shift(x, by):
        places = len(RING)
        pairs = [
            ((RING[p] * 2 + i) * 2 + core, (RING[(p + (1 - 2 * core) * by) % places] * 2 + i) * 2 + core)
            for p in range(places)
            for i in range(2)
            for core in range(2)
        ]
        return lax.ppermute(x, ("ctx", "batch"), pairs)

    def swap(x):
        return lax.ppermute(x, "ctx", [(i, i ^ 1) for i in range(count)])

    def pick(step, line):
        body = functools.partial(pick_kernel, step, width, top)
        return call(body, shape((low + rows, rows), BF16), [VMEM] * 2, moved=2 * 10**6)(asked, line)

    own = jnp.concatenate([pages, index_keys[0]], axis=0)
    below = shift(own, 1)
    near = swap(own)
    above = shift(own, -1)
    asked = swap(block_list[0])
    query_count = tile_len * head_count
    index_rows = index_q[0].reshape(-1, index_q.shape[3])
    q_rows, fresh, new_rows = call(
        prepare_kernel,
        (shape((query_count, width), BF16), shape((query_count, 128), F32), shape((128, latent), BF16)),
        [VMEM] * 2,
        (VMEM,) * 3,
        [pltpu.VMEM((128, width), BF16)],
        moved=4 * query_count * width,
    )(query, kv_new[0])
    below, asked, q_rows, fresh = lax.optimization_barrier((below, asked, q_rows, fresh))
    far = shift(below, 1)
    asked, near = lax.optimization_barrier((asked, near))
    side_below = swap(pick(0, below))
    side_above = swap(pick(1, above))
    side_far = swap(pick(2, far))
    sums = pltpu.VMEM((2 * count, index_rows.shape[0]), F32)
    columns = chosen.shape[0] * BLK
    score, turned, key_rows, marks = call(
        functools.partial(early_kernel, width, latent, top),
        (shape((tile_len, 2 * count), F32), shape((width, columns), BF16), shape((columns, latent), BF16), shape((8, columns), jnp.int32)),
        [SMEM] * 2 + [VMEM] * 9,
        (VMEM,) * 4,
        [pltpu.VMEM((8, width, rows), BF16), sums],
        moved=4 * query_count * width,
    )(chosen, context_len, index_weight[0], index_rows, own, near, below, above, far, side_below, side_above)
    chunk = query_count // 2
    attended, block_score = call(
        functools.partial(attend_kernel, width, latent, top, chunk),
        (shape((query_count, latent), BF16), shape((tile_len, 2 * count), F32)),
        [VMEM] * 10,
        (ANY, ANY),
        [
            pltpu.VMEM((width, columns), BF16),
            pltpu.VMEM((columns, latent), BF16),
            sums,
            pltpu.VMEM((query_count, latent), BF16),
            pltpu.VMEM((tile_len, 2 * count), F32),
            pltpu.SemaphoreType.DMA((2 + 1,)),
        ],
    )(q_rows, fresh, new_rows, turned, key_rows, marks, score, side_far, index_weight[0], index_rows)
    return attended.reshape(1, tile_len, head_count, latent), block_score[None]


def on_device(
    q_latent, kv_new, kv_cache, index_q, index_weight, index_keys, block_list, context_len
):
    ctx_count = lax.axis_size("ctx")
    my_index = lax.axis_index("ctx")
    tile_len = q_latent.shape[1]
    head_count = q_latent.shape[2]
    row_width = q_latent.shape[3]
    latent_width = row_width - DR
    ctx_rows = kv_cache.shape[1]
    blocks_dev = ctx_rows // BLK
    block_total = blocks_dev * ctx_count
    index_heads = index_q.shape[2]
    index_width = index_q.shape[3]
    length = context_len[0]
    head_weight = index_weight[0]
    index_rows = index_q[0].reshape(tile_len * index_heads, index_width)
    weight_f32 = head_weight.astype(jnp.float32)
    piece = lax.all_gather(index_keys[0], "ctx", axis=0, tiled=True)
    count = piece.shape[0]
    products = jnp.dot(index_rows, piece.T, preferred_element_type=jnp.float32)
    activ = jnp.maximum(products, 0.0).reshape(tile_len, index_heads, count)
    weighted = jnp.einsum("tjr,tj->tr", activ, weight_f32, precision=lax.Precision.HIGHEST)
    positions = jnp.arange(count)
    weighted = jnp.where(positions[None, :] < length, weighted, 0.0)
    summed = jax.ops.segment_sum(weighted.T, positions // BLK, num_segments=block_total)
    block_sums = summed.T
    block_score = (block_sums / BLK).reshape(1, tile_len, block_total)
    all_lists = lax.all_gather(block_list[0], "ctx", axis=0, tiled=True)
    is_mine = all_lists // blocks_dev == my_index
    slot_index = jnp.sum(jnp.where(is_mine, all_lists % blocks_dev, 0), axis=1)
    wanted = jnp.any(is_mine, axis=1)
    own_blocks = kv_cache[0].reshape(blocks_dev, BLK, row_width)
    outgoing = jnp.where(wanted[:, None, None], own_blocks[slot_index], jnp.zeros((), jnp.bfloat16))
    incoming = lax.all_to_all(outgoing, "ctx", split_axis=0, concat_axis=0, tiled=True)
    chosen = block_list[0, 0]
    cached_rows = incoming[chosen // blocks_dev].reshape(-1, row_width)
    positions = (chosen[:, None] * BLK + jnp.arange(BLK)[None, :]).reshape(-1)
    key_rows = jnp.concatenate([cached_rows, kv_new[0]], axis=0)
    query_rows = q_latent[0].reshape(tile_len * head_count, row_width)
    scores = jnp.dot(query_rows, key_rows.T, preferred_element_type=jnp.float32) * softmax_scale
    cache_ok = positions < length
    token_of = jnp.arange(tile_len * head_count) // head_count
    new_ok = jnp.arange(tile_len)[None, :] <= token_of[:, None]
    allowed = jnp.concatenate(
        [
            jnp.broadcast_to(cache_ok[None, :], (tile_len * head_count, cached_rows.shape[0])),
            new_ok,
        ],
        axis=1,
    )
    scores = jnp.where(allowed, scores, neg_fill)
    highest = jnp.max(scores, axis=1, keepdims=True)
    expo = jnp.exp(scores - highest)
    total = jnp.sum(expo, axis=1, keepdims=True)
    probs = expo.astype(jnp.bfloat16)
    mixed = jnp.dot(probs, key_rows[:, :latent_width], preferred_element_type=jnp.float32) / total
    attended = mixed.astype(jnp.bfloat16).reshape(1, tile_len, head_count, latent_width)
    return (attended, block_score)


def solution(mesh):
    placed = (
        P(("groups", "batch"), "ctx", None, None),
        P(("groups", "batch"), "ctx", None),
        P(("groups", "batch"), "ctx", None),
        P(("groups", "batch"), "ctx", None, None),
        P(("groups", "batch"), "ctx", None),
        P(("groups", "batch"), "ctx", None),
        P(("groups", "batch"), "ctx", None),
        P(("groups", "batch")),
    )
    return jax.shard_map(
        on_ring if mesh.shape["ctx"] == 8 else on_device,
        mesh=mesh,
        in_specs=placed,
        out_specs=(P(("groups", "batch"), "ctx", None, None), P(("groups", "batch"), "ctx", None)),
        check_vma=False,
    )
```

```python
import functools
import math

import jax
import jax.numpy as jnp
from jax import lax
from jax.experimental import pallas as pl
from jax.experimental.pallas import tpu as pltpu
from jax.sharding import PartitionSpec as P

DR = 64
BLK = 64


softmax_scale = 0.07216878364870322
neg_fill = -1e30
F32 = jnp.float32
BF16 = jnp.bfloat16


def nt_dot(a, b):
    return lax.dot_general(a, b, (((1,), (1,)), ((), ())), preferred_element_type=F32)


def turn(x):
    return jnp.concatenate([x[:, BLK:], x[:, :BLK]], axis=1)


RING = (0, 2, 3, 1)


def ring_steps(me):
    level = me // 2
    odd = jnp.bitwise_xor(level, level // 2) % 2 != lax.axis_index("batch")
    return jnp.where(odd, 4, 2), jnp.where(odd, 2, 4), 6


def pick_kernel(step, width, top, list_ref, line_ref, out_ref):
    me = lax.axis_index("ctx")
    holder = jnp.bitwise_xor(me, ring_steps(me)[step])
    asked = jnp.where(list_ref[...] == 2 * holder + 1, 1.0, 0.0)
    upper = jnp.max(asked, axis=1, keepdims=True) > 0.5
    low = width - top
    rows = 2 * BLK
    lane = lax.broadcasted_iota(jnp.int32, (1, rows), 1)
    first = line_ref[0:low, :].astype(F32)
    second = line_ref[top:width, :].astype(F32)
    first = jnp.where(upper, turn(first), first)
    second = jnp.where(upper, second, turn(second))
    out_ref[0:low, :] = jnp.where(lane < BLK, first, second).astype(BF16)
    out_ref[low : low + rows, :] = line_ref[width : width + rows, :]


def prepare_kernel(q_ref, new_ref, rows_ref, scores_ref, new_rows_ref, wide_ref):
    tokens, _, heads = q_ref.shape
    padding = jnp.zeros((wide_ref.shape[0] - tokens, wide_ref.shape[1]), F32)
    wide = jnp.concatenate([new_ref[...].astype(F32), padding], axis=0).astype(BF16)
    wide_ref[...] = wide
    new_rows_ref[...] = wide[:, 0 : new_rows_ref.shape[1]]
    column = lax.broadcasted_iota(jnp.int32, (1, wide_ref.shape[0]), 1)
    for t in range(tokens):
        rows_ref[t * heads : (t + 1) * heads, :] = q_ref[t].T
    scores = nt_dot(rows_ref[...], wide_ref[...])
    for t in range(tokens):
        place = slice(t * heads, (t + 1) * heads)
        scores_ref[place, :] = jnp.where(column <= t, scores[place, :], neg_fill)


def page_sums(keys, query, room, holder, sums):
    rows = 2 * BLK
    row = lax.broadcasted_iota(jnp.int32, (rows, rows), 0)
    keys = jnp.where(row < room, keys, jnp.zeros((), BF16))
    activ = jnp.maximum(nt_dot(keys, query), 0.0)
    sums[pl.ds(2 * holder, 1), :] = jnp.sum(activ[0:BLK, :], axis=0, keepdims=True)
    sums[pl.ds(2 * holder + 1, 1), :] = jnp.sum(activ[BLK:rows, :], axis=0, keepdims=True)


def weigh(weight_ref, sums):
    weight = weight_ref[...].astype(F32)
    tokens, heads = weight.shape
    total = sums.shape[1]
    lane = lax.broadcasted_iota(jnp.int32, (tokens, total), 1)
    token = lax.broadcasted_iota(jnp.int32, (tokens, total), 0)
    wide = jnp.where(lane // heads == token, jnp.concatenate([weight] * tokens, axis=1), 0.0)
    score = lax.dot_general(
        wide, sums[...], (((1,), (1,)), ((), ())), precision=lax.Precision.HIGHEST, preferred_element_type=F32
    )
    return score * (1.0 / BLK)


def early_kernel(
    width, latent, top, list_ref, length_ref, weight_ref, query_ref,
    own, near, below, above, far, side_below, side_above,
    score_ref, turned_ref, rows_ref, marks_ref, slots, sums,
):
    me = lax.axis_index("ctx")
    behind, ahead, opposite = ring_steps(me)
    last = jnp.bitwise_xor(me, opposite + 1)
    low = width - top
    rows = 2 * BLK
    lane = lax.broadcasted_iota(jnp.int32, (1, rows), 1)
    for slot, ref in ((0, own), (1, near), (behind, below), (ahead, above), (opposite, far)):
        slots[slot] = ref[0:width, :]
    for slot, ref in ((behind + 1, side_below), (ahead + 1, side_above)):
        slots[slot, 0:top, :] = ref[0:top, :]
        slots[slot, top:width, :] = turn(ref[0:low, :].astype(F32)).astype(BF16)
    slots[opposite + 1] = jnp.zeros((width, rows), BF16)
    column = lax.broadcasted_iota(jnp.int32, (1, list_ref.shape[0] * BLK), 1)
    limit = jnp.zeros_like(column)
    late = jnp.zeros_like(column)
    length = length_ref[0]
    pages = list_ref.shape[0]
    for pair in range(pages // 2):
        halves = []
        for j in (2 * pair, 2 * pair + 1):
            page = list_ref[j]
            holder, half = page // 2, lax.rem(page, 2)
            slot = jnp.bitwise_xor(holder, me)
            high = jnp.where((slot == 1) | (lax.rem(slot, 2) == 0), half, 0)
            block = slots[slot].astype(F32)
            halves.append(jnp.where(high == j - 2 * pair, block, turn(block)))
            limit = jnp.where(column // BLK == j, length - page * BLK + j * BLK, limit)
            late = jnp.where((column // BLK == j) & (holder == last), 1, late)
        block = jnp.where(lane < BLK, halves[0], halves[1]).astype(BF16)
        place = slice(pair * rows, (pair + 1) * rows)
        turned_ref[:, place] = block
        rows_ref[place, :] = block[0:latent, :].T
    marks_ref[0:1, :] = limit
    marks_ref[1:2, :] = late
    marks_ref[2:3, :] = jnp.full_like(column, length - last * rows)
    query = query_ref[...]
    sums[pl.ds(2 * last, 1), :] = jnp.zeros((1, sums.shape[1]), F32)
    sums[pl.ds(2 * last + 1, 1), :] = jnp.zeros((1, sums.shape[1]), F32)
    for ref, start, step in (
        (own, width, 0),
        (near, width, 1),
        (below, width, behind),
        (above, width, ahead),
        (far, width, opposite),
        (side_below, low, behind + 1),
        (side_above, low, ahead + 1),
    ):
        holder = jnp.bitwise_xor(me, step)
        page_sums(ref[start : start + rows, :], query, length - holder * rows, holder, sums)
    score_ref[...] = weigh(weight_ref, sums)


def attend_kernel(
    width, latent, top, chunk, q_ref, fresh_ref, new_rows, early_turned, early_rows, marks_ref, early_score, side_far,
    weight_ref, query_ref,
    out_hbm, score_hbm, turned, key_rows, sums, out_ref, score_ref, sems,
):
    last = jnp.bitwise_xor(lax.axis_index("ctx"), 7)
    low = width - top
    rows = 2 * BLK
    sums[...] = jnp.zeros_like(sums)
    page_sums(side_far[low : low + rows, :], query_ref[...], marks_ref[2:3, 0:rows], last, sums)
    score_ref[...] = early_score[...] + weigh(weight_ref, sums)
    steps = q_ref.shape[0] // chunk
    copies = [pltpu.make_async_copy(score_ref, score_hbm, sems.at[steps])]
    copies[0].start()
    lane = lax.broadcasted_iota(jnp.int32, (1, rows), 1)
    packed = side_far[0:low, :].astype(F32)
    swapped = turn(packed)
    first = jnp.concatenate([packed[0:top], swapped], axis=0)
    second = jnp.concatenate([swapped[0:top], packed], axis=0)
    both = jnp.where(lane < BLK, first, second).astype(BF16)
    both_rows = both[0:latent, :].T
    limit = marks_ref[0:1, :]
    late = marks_ref[1:2, :]
    for place in range(0, turned.shape[1], rows):
        place = slice(place, place + rows)
        turned[:, place] = jnp.where(late[:, place] == 1, both, early_turned[:, place])
        down = jnp.broadcast_to(late[:, place].astype(F32), (rows, rows)).T[:, 0:1]
        key_rows[place, :] = jnp.where(down > 0.5, both_rows, early_rows[place, :])
    factor = softmax_scale * math.log2(math.e)
    column = lax.broadcasted_iota(jnp.int32, (1, turned.shape[1]), 1)
    for step in range(steps):
        place = slice(step * chunk, (step + 1) * chunk)
        scores = jnp.dot(q_ref[place, :], turned[...], preferred_element_type=F32)
        scores = jnp.where(column < limit, scores, neg_fill)
        fresh = fresh_ref[place, :]
        highest = jnp.maximum(jnp.max(scores, axis=1, keepdims=True), jnp.max(fresh, axis=1, keepdims=True))
        expo = jnp.exp2((scores - highest) * factor)
        expo_new = jnp.exp2((fresh - highest) * factor)
        total = jnp.sum(expo, axis=1, keepdims=True) + jnp.sum(expo_new, axis=1, keepdims=True)
        probs = jnp.concatenate([expo.astype(BF16), expo_new.astype(BF16)], axis=1)
        values = jnp.concatenate([key_rows[...], new_rows[...]], axis=0)
        mixed = jnp.dot(probs, values, preferred_element_type=F32)
        out_ref[place, :] = (mixed / total).astype(BF16)
        copies.append(pltpu.make_async_copy(out_ref.at[place], out_hbm.at[place], sems.at[step]))
        copies[-1].start()
    for copy in copies:
        copy.wait()


VMEM = pl.BlockSpec(memory_space=pltpu.VMEM)
SMEM = pl.BlockSpec(memory_space=pltpu.SMEM)
ANY = pl.BlockSpec(memory_space=pl.ANY)


def call(body, shapes, in_specs, out_specs=VMEM, scratch=(), moved=0):
    return pl.pallas_call(
        body,
        out_shape=shapes,
        in_specs=in_specs,
        out_specs=out_specs,
        scratch_shapes=scratch,
        cost_estimate=pl.CostEstimate(flops=0, bytes_accessed=moved, transcendentals=0),
        compiler_params=pltpu.CompilerParams(vmem_limit_bytes=32 * 1024 * 1024),
    )


def on_ring(
    q_latent, kv_new, kv_cache, index_q, index_weight, index_keys, block_list, context_len
):
    count = lax.axis_size("ctx")
    tile_len, head_count, width = q_latent.shape[1:]
    latent = width - DR
    rows = kv_cache.shape[1]
    chosen = block_list[0, 0]
    top = 256
    low = width - top
    pages = kv_cache[0].T
    query = jnp.transpose(q_latent[0], (0, 2, 1))
    shape = jax.ShapeDtypeStruct

    def shift(x, by):
        places = len(RING)
        pairs = [
            ((RING[p] * 2 + i) * 2 + core, (RING[(p + (1 - 2 * core) * by) % places] * 2 + i) * 2 + core)
            for p in range(places)
            for i in range(2)
            for core in range(2)
        ]
        return lax.ppermute(x, ("ctx", "batch"), pairs)

    def swap(x):
        return lax.ppermute(x, "ctx", [(i, i ^ 1) for i in range(count)])

    def pick(step, line):
        body = functools.partial(pick_kernel, step, width, top)
        return call(body, shape((low + rows, rows), BF16), [VMEM] * 2, moved=2 * 10**6)(asked, line)

    own = jnp.concatenate([pages, index_keys[0]], axis=0)
    below = shift(own, 1)
    near = swap(own)
    above = shift(own, -1)
    asked = swap(block_list[0])
    query_count = tile_len * head_count
    index_rows = index_q[0].reshape(-1, index_q.shape[3])
    q_rows, fresh, new_rows = call(
        prepare_kernel,
        (shape((query_count, width), BF16), shape((query_count, 128), F32), shape((128, latent), BF16)),
        [VMEM] * 2,
        (VMEM,) * 3,
        [pltpu.VMEM((128, width), BF16)],
        moved=4 * query_count * width,
    )(query, kv_new[0])
    below, asked, q_rows, fresh = lax.optimization_barrier((below, asked, q_rows, fresh))
    far = shift(below, 1)
    asked, near = lax.optimization_barrier((asked, near))
    side_below = swap(pick(0, below))
    side_above = swap(pick(1, above))
    side_far = swap(pick(2, far))
    sums = pltpu.VMEM((2 * count, index_rows.shape[0]), F32)
    columns = chosen.shape[0] * BLK
    score, turned, key_rows, marks = call(
        functools.partial(early_kernel, width, latent, top),
        (shape((tile_len, 2 * count), F32), shape((width, columns), BF16), shape((columns, latent), BF16), shape((8, columns), jnp.int32)),
        [SMEM] * 2 + [VMEM] * 9,
        (VMEM,) * 4,
        [pltpu.VMEM((8, width, rows), BF16), sums],
        moved=4 * query_count * width,
    )(chosen, context_len, index_weight[0], index_rows, own, near, below, above, far, side_below, side_above)
    chunk = query_count // 2
    attended, block_score = call(
        functools.partial(attend_kernel, width, latent, top, chunk),
        (shape((query_count, latent), BF16), shape((tile_len, 2 * count), F32)),
        [VMEM] * 10,
        (ANY, ANY),
        [
            pltpu.VMEM((width, columns), BF16),
            pltpu.VMEM((columns, latent), BF16),
            sums,
            pltpu.VMEM((query_count, latent), BF16),
            pltpu.VMEM((tile_len, 2 * count), F32),
            pltpu.SemaphoreType.DMA((3,)),
        ],
    )(q_rows, fresh, new_rows, turned, key_rows, marks, score, side_far, index_weight[0], index_rows)
    return attended.reshape(1, tile_len, head_count, latent), block_score[None]


def on_device(
    q_latent, kv_new, kv_cache, index_q, index_weight, index_keys, block_list, context_len
):
    ctx_count = lax.axis_size("ctx")
    my_index = lax.axis_index("ctx")
    tile_len = q_latent.shape[1]
    head_count = q_latent.shape[2]
    row_width = q_latent.shape[3]
    latent_width = row_width - DR
    ctx_rows = kv_cache.shape[1]
    blocks_dev = ctx_rows // BLK
    block_total = blocks_dev * ctx_count
    index_heads = index_q.shape[2]
    index_width = index_q.shape[3]
    length = context_len[0]
    head_weight = index_weight[0]
    index_rows = index_q[0].reshape(tile_len * index_heads, index_width)
    weight_f32 = head_weight.astype(jnp.float32)
    piece = lax.all_gather(index_keys[0], "ctx", axis=0, tiled=True)
    count = piece.shape[0]
    products = jnp.dot(index_rows, piece.T, preferred_element_type=jnp.float32)
    activ = jnp.maximum(products, 0.0).reshape(tile_len, index_heads, count)
    weighted = jnp.einsum("tjr,tj->tr", activ, weight_f32, precision=lax.Precision.HIGHEST)
    positions = jnp.arange(count)
    weighted = jnp.where(positions[None, :] < length, weighted, 0.0)
    summed = jax.ops.segment_sum(weighted.T, positions // BLK, num_segments=block_total)
    block_sums = summed.T
    block_score = (block_sums / BLK).reshape(1, tile_len, block_total)
    all_lists = lax.all_gather(block_list[0], "ctx", axis=0, tiled=True)
    is_mine = all_lists // blocks_dev == my_index
    slot_index = jnp.sum(jnp.where(is_mine, all_lists % blocks_dev, 0), axis=1)
    wanted = jnp.any(is_mine, axis=1)
    own_blocks = kv_cache[0].reshape(blocks_dev, BLK, row_width)
    outgoing = jnp.where(wanted[:, None, None], own_blocks[slot_index], jnp.zeros((), jnp.bfloat16))
    incoming = lax.all_to_all(outgoing, "ctx", split_axis=0, concat_axis=0, tiled=True)
    chosen = block_list[0, 0]
    cached_rows = incoming[chosen // blocks_dev].reshape(-1, row_width)
    positions = (chosen[:, None] * BLK + jnp.arange(BLK)[None, :]).reshape(-1)
    key_rows = jnp.concatenate([cached_rows, kv_new[0]], axis=0)
    query_rows = q_latent[0].reshape(tile_len * head_count, row_width)
    scores = jnp.dot(query_rows, key_rows.T, preferred_element_type=jnp.float32) * softmax_scale
    cache_ok = positions < length
    token_of = jnp.arange(tile_len * head_count) // head_count
    new_ok = jnp.arange(tile_len)[None, :] <= token_of[:, None]
    allowed = jnp.concatenate(
        [
            jnp.broadcast_to(cache_ok[None, :], (tile_len * head_count, cached_rows.shape[0])),
            new_ok,
        ],
        axis=1,
    )
    scores = jnp.where(allowed, scores, neg_fill)
    highest = jnp.max(scores, axis=1, keepdims=True)
    expo = jnp.exp(scores - highest)
    total = jnp.sum(expo, axis=1, keepdims=True)
    probs = expo.astype(jnp.bfloat16)
    mixed = jnp.dot(probs, key_rows[:, :latent_width], preferred_element_type=jnp.float32) / total
    attended = mixed.astype(jnp.bfloat16).reshape(1, tile_len, head_count, latent_width)
    return (attended, block_score)


def solution(mesh):
    placed = (
        P(("groups", "batch"), "ctx", None, None),
        P(("groups", "batch"), "ctx", None),
        P(("groups", "batch"), "ctx", None),
        P(("groups", "batch"), "ctx", None, None),
        P(("groups", "batch"), "ctx", None),
        P(("groups", "batch"), "ctx", None),
        P(("groups", "batch"), "ctx", None),
        P(("groups", "batch")),
    )
    return jax.shard_map(
        on_ring if mesh.shape["ctx"] == 8 and mesh.shape["batch"] == 2 else on_device,
        mesh=mesh,
        in_specs=placed,
        out_specs=(P(("groups", "batch"), "ctx", None, None), P(("groups", "batch"), "ctx", None)),
        check_vma=False,
    )
```

```python
import functools
import math

import jax
import jax.numpy as jnp
from jax import lax
from jax.experimental import pallas as pl
from jax.experimental.pallas import tpu as pltpu
from jax.sharding import PartitionSpec as P

DR = 64
BLK = 64


softmax_scale = 0.07216878364870322
neg_fill = -1e30
F32 = jnp.float32
BF16 = jnp.bfloat16


def nt_dot(a, b):
    return lax.dot_general(a, b, (((1,), (1,)), ((), ())), preferred_element_type=F32)


def turn(x):
    return jnp.concatenate([x[:, BLK:], x[:, :BLK]], axis=1)


RING = (0, 2, 3, 1)


def ring_steps(me):
    level = me // 2
    odd = jnp.bitwise_xor(level, level // 2) % 2 != lax.axis_index("batch")
    return jnp.where(odd, 4, 2), jnp.where(odd, 2, 4), 6


def pick_kernel(step, width, top, list_ref, line_ref, out_ref):
    me = lax.axis_index("ctx")
    holder = jnp.bitwise_xor(me, ring_steps(me)[step])
    asked = jnp.where(list_ref[...] == 2 * holder + 1, 1.0, 0.0)
    upper = jnp.max(asked, axis=1, keepdims=True) > 0.5
    low = width - top
    rows = 2 * BLK
    lane = lax.broadcasted_iota(jnp.int32, (1, rows), 1)
    first = line_ref[0:low, :].astype(F32)
    second = line_ref[top:width, :].astype(F32)
    first = jnp.where(upper, turn(first), first)
    second = jnp.where(upper, second, turn(second))
    out_ref[0:low, :] = jnp.where(lane < BLK, first, second).astype(BF16)
    out_ref[low : low + rows, :] = line_ref[width : width + rows, :]


def prepare_kernel(q_ref, new_ref, rows_ref, scores_ref, new_rows_ref, wide_ref):
    tokens, _, heads = q_ref.shape
    padding = jnp.zeros((wide_ref.shape[0] - tokens, wide_ref.shape[1]), F32)
    wide = jnp.concatenate([new_ref[...].astype(F32), padding], axis=0).astype(BF16)
    wide_ref[...] = wide
    new_rows_ref[...] = wide[:, 0 : new_rows_ref.shape[1]]
    column = lax.broadcasted_iota(jnp.int32, (1, wide_ref.shape[0]), 1)
    for t in range(tokens):
        rows_ref[t * heads : (t + 1) * heads, :] = q_ref[t].T
    scores = nt_dot(rows_ref[...], wide_ref[...])
    for t in range(tokens):
        place = slice(t * heads, (t + 1) * heads)
        scores_ref[place, :] = jnp.where(column <= t, scores[place, :], neg_fill)


def page_sums(keys, query, room, holder, sums):
    rows = 2 * BLK
    row = lax.broadcasted_iota(jnp.int32, (rows, rows), 0)
    keys = jnp.where(row < room, keys, jnp.zeros((), BF16))
    activ = jnp.maximum(nt_dot(keys, query), 0.0)
    sums[pl.ds(2 * holder, 1), :] = jnp.sum(activ[0:BLK, :], axis=0, keepdims=True)
    sums[pl.ds(2 * holder + 1, 1), :] = jnp.sum(activ[BLK:rows, :], axis=0, keepdims=True)


def weigh(weight_ref, sums):
    weight = weight_ref[...].astype(F32)
    tokens, heads = weight.shape
    total = sums.shape[1]
    lane = lax.broadcasted_iota(jnp.int32, (tokens, total), 1)
    token = lax.broadcasted_iota(jnp.int32, (tokens, total), 0)
    wide = jnp.where(lane // heads == token, jnp.concatenate([weight] * tokens, axis=1), 0.0)
    score = lax.dot_general(
        wide, sums[...], (((1,), (1,)), ((), ())), precision=lax.Precision.HIGHEST, preferred_element_type=F32
    )
    return score * (1.0 / BLK)


def early_kernel(
    width, latent, top, list_ref, length_ref, weight_ref, query_ref,
    own, near, below, above, far, side_below, side_above,
    score_ref, turned_ref, rows_ref, marks_ref, slots, sums,
):
    me = lax.axis_index("ctx")
    behind, ahead, opposite = ring_steps(me)
    last = jnp.bitwise_xor(me, opposite + 1)
    low = width - top
    rows = 2 * BLK
    lane = lax.broadcasted_iota(jnp.int32, (1, rows), 1)
    for slot, ref in ((0, own), (1, near), (behind, below), (ahead, above), (opposite, far)):
        slots[slot] = ref[0:width, :]
    for slot, ref in ((behind + 1, side_below), (ahead + 1, side_above)):
        slots[slot, 0:top, :] = ref[0:top, :]
        slots[slot, top:width, :] = turn(ref[0:low, :].astype(F32)).astype(BF16)
    slots[opposite + 1] = jnp.zeros((width, rows), BF16)
    column = lax.broadcasted_iota(jnp.int32, (1, list_ref.shape[0] * BLK), 1)
    limit = jnp.zeros_like(column)
    late = jnp.zeros_like(column)
    length = length_ref[0]
    pages = list_ref.shape[0]
    for pair in range(pages // 2):
        halves = []
        for j in (2 * pair, 2 * pair + 1):
            page = list_ref[j]
            holder, half = page // 2, lax.rem(page, 2)
            slot = jnp.bitwise_xor(holder, me)
            high = jnp.where((slot == 1) | (lax.rem(slot, 2) == 0), half, 0)
            block = slots[slot].astype(F32)
            halves.append(jnp.where(high == j - 2 * pair, block, turn(block)))
            limit = jnp.where(column // BLK == j, length - page * BLK + j * BLK, limit)
            late = jnp.where((column // BLK == j) & (holder == last), 1, late)
        block = jnp.where(lane < BLK, halves[0], halves[1]).astype(BF16)
        place = slice(pair * rows, (pair + 1) * rows)
        turned_ref[:, place] = block
        rows_ref[place, :] = block[0:latent, :].T
    marks_ref[0:1, :] = limit
    marks_ref[1:2, :] = late
    marks_ref[2:3, :] = jnp.full_like(column, length - last * rows)
    query = query_ref[...]
    sums[pl.ds(2 * last, 1), :] = jnp.zeros((1, sums.shape[1]), F32)
    sums[pl.ds(2 * last + 1, 1), :] = jnp.zeros((1, sums.shape[1]), F32)
    for ref, start, step in (
        (own, width, 0),
        (near, width, 1),
        (below, width, behind),
        (above, width, ahead),
        (far, width, opposite),
        (side_below, low, behind + 1),
        (side_above, low, ahead + 1),
    ):
        holder = jnp.bitwise_xor(me, step)
        page_sums(ref[start : start + rows, :], query, length - holder * rows, holder, sums)
    score_ref[...] = weigh(weight_ref, sums)


def attend_kernel(
    width, latent, top, chunk, q_ref, fresh_ref, new_rows, early_turned, early_rows, marks_ref, early_score, side_far,
    weight_ref, query_ref,
    out_hbm, score_hbm, turned, key_rows, sums, out_ref, score_ref, sems,
):
    last = jnp.bitwise_xor(lax.axis_index("ctx"), 7)
    low = width - top
    rows = 2 * BLK
    sums[...] = jnp.zeros_like(sums)
    page_sums(side_far[low : low + rows, :], query_ref[...], marks_ref[2:3, 0:rows], last, sums)
    score_ref[...] = early_score[...] + weigh(weight_ref, sums)
    steps = q_ref.shape[0] // chunk
    copies = [pltpu.make_async_copy(score_ref, score_hbm, sems.at[steps])]
    copies[0].start()
    lane = lax.broadcasted_iota(jnp.int32, (1, rows), 1)
    packed = side_far[0:low, :].astype(F32)
    swapped = turn(packed)
    first = jnp.concatenate([packed[0:top], swapped], axis=0)
    second = jnp.concatenate([swapped[0:top], packed], axis=0)
    both = jnp.where(lane < BLK, first, second).astype(BF16)
    both_rows = both[0:latent, :].T
    limit = marks_ref[0:1, :]
    late = marks_ref[1:2, :]
    for place in range(0, turned.shape[1], rows):
        place = slice(place, place + rows)
        turned[:, place] = jnp.where(late[:, place] == 1, both, early_turned[:, place])
        down = jnp.broadcast_to(late[:, place].astype(F32), (rows, rows)).T[:, 0:1]
        key_rows[place, :] = jnp.where(down > 0.5, both_rows, early_rows[place, :])
    factor = softmax_scale * math.log2(math.e)
    column = lax.broadcasted_iota(jnp.int32, (1, turned.shape[1]), 1)
    for step in range(steps):
        place = slice(step * chunk, (step + 1) * chunk)
        scores = jnp.dot(q_ref[place, :], turned[...], preferred_element_type=F32)
        scores = jnp.where(column < limit, scores, neg_fill)
        fresh = fresh_ref[place, :]
        highest = jnp.maximum(jnp.max(scores, axis=1, keepdims=True), jnp.max(fresh, axis=1, keepdims=True))
        expo = jnp.exp2((scores - highest) * factor)
        expo_new = jnp.exp2((fresh - highest) * factor)
        total = jnp.sum(expo, axis=1, keepdims=True) + jnp.sum(expo_new, axis=1, keepdims=True)
        probs = jnp.concatenate([expo.astype(BF16), expo_new.astype(BF16)], axis=1)
        values = jnp.concatenate([key_rows[...], new_rows[...]], axis=0)
        mixed = jnp.dot(probs, values, preferred_element_type=F32)
        out_ref[place, :] = (mixed / total).astype(BF16)
        copies.append(pltpu.make_async_copy(out_ref.at[place], out_hbm.at[place], sems.at[step]))
        copies[-1].start()
    for copy in copies:
        copy.wait()


VMEM = pl.BlockSpec(memory_space=pltpu.VMEM)
SMEM = pl.BlockSpec(memory_space=pltpu.SMEM)
ANY = pl.BlockSpec(memory_space=pl.ANY)


def call(body, shapes, in_specs, out_specs=VMEM, scratch=(), moved=0):
    return pl.pallas_call(
        body,
        out_shape=shapes,
        in_specs=in_specs,
        out_specs=out_specs,
        scratch_shapes=scratch,
        cost_estimate=pl.CostEstimate(flops=0, bytes_accessed=moved, transcendentals=0),
        compiler_params=pltpu.CompilerParams(vmem_limit_bytes=32 * 1024 * 1024),
    )


def on_ring(
    q_latent, kv_new, kv_cache, index_q, index_weight, index_keys, block_list, context_len
):
    count = lax.axis_size("ctx")
    tile_len, head_count, width = q_latent.shape[1:]
    latent = width - DR
    rows = kv_cache.shape[1]
    chosen = block_list[0, 0]
    top = width // 2
    low = width - top
    pages = kv_cache[0].T
    query = jnp.transpose(q_latent[0], (0, 2, 1))
    shape = jax.ShapeDtypeStruct

    def shift(x, by):
        places = len(RING)
        pairs = [
            ((RING[p] * 2 + i) * 2 + core, (RING[(p + (1 - 2 * core) * by) % places] * 2 + i) * 2 + core)
            for p in range(places)
            for i in range(2)
            for core in range(2)
        ]
        return lax.ppermute(x, ("ctx", "batch"), pairs)

    def swap(x):
        return lax.ppermute(x, "ctx", [(i, i ^ 1) for i in range(count)])

    def pick(step, line):
        body = functools.partial(pick_kernel, step, width, top)
        return call(body, shape((low + rows, rows), BF16), [VMEM] * 2, moved=2 * 10**6)(asked, line)

    own = jnp.concatenate([pages, index_keys[0]], axis=0)
    below = shift(own, 1)
    near = swap(own)
    above = shift(own, -1)
    asked = swap(block_list[0])
    query_count = tile_len * head_count
    index_rows = index_q[0].reshape(-1, index_q.shape[3])
    q_rows, fresh, new_rows = call(
        prepare_kernel,
        (shape((query_count, width), BF16), shape((query_count, 128), F32), shape((128, latent), BF16)),
        [VMEM] * 2,
        (VMEM,) * 3,
        [pltpu.VMEM((128, width), BF16)],
        moved=4 * query_count * width,
    )(query, kv_new[0])
    below, asked, q_rows, fresh = lax.optimization_barrier((below, asked, q_rows, fresh))
    far = shift(below, 1)
    asked, near = lax.optimization_barrier((asked, near))
    side_below = swap(pick(0, below))
    side_above = swap(pick(1, above))
    side_far = swap(pick(2, far))
    sums = pltpu.VMEM((2 * count, index_rows.shape[0]), F32)
    columns = chosen.shape[0] * BLK
    score, turned, key_rows, marks = call(
        functools.partial(early_kernel, width, latent, top),
        (shape((tile_len, 2 * count), F32), shape((width, columns), BF16), shape((columns, latent), BF16), shape((8, columns), jnp.int32)),
        [SMEM] * 2 + [VMEM] * 9,
        (VMEM,) * 4,
        [pltpu.VMEM((8, width, rows), BF16), sums],
        moved=4 * query_count * width,
    )(chosen, context_len, index_weight[0], index_rows, own, near, below, above, far, side_below, side_above)
    chunk = query_count // 2
    attended, block_score = call(
        functools.partial(attend_kernel, width, latent, top, chunk),
        (shape((query_count, latent), BF16), shape((tile_len, 2 * count), F32)),
        [VMEM] * 10,
        (ANY, ANY),
        [
            pltpu.VMEM((width, columns), BF16),
            pltpu.VMEM((columns, latent), BF16),
            sums,
            pltpu.VMEM((query_count, latent), BF16),
            pltpu.VMEM((tile_len, 2 * count), F32),
            pltpu.SemaphoreType.DMA((3,)),
        ],
    )(q_rows, fresh, new_rows, turned, key_rows, marks, score, side_far, index_weight[0], index_rows)
    return attended.reshape(1, tile_len, head_count, latent), block_score[None]


def on_device(
    q_latent, kv_new, kv_cache, index_q, index_weight, index_keys, block_list, context_len
):
    ctx_count = lax.axis_size("ctx")
    my_index = lax.axis_index("ctx")
    tile_len = q_latent.shape[1]
    head_count = q_latent.shape[2]
    row_width = q_latent.shape[3]
    latent_width = row_width - DR
    ctx_rows = kv_cache.shape[1]
    blocks_dev = ctx_rows // BLK
    block_total = blocks_dev * ctx_count
    index_heads = index_q.shape[2]
    index_width = index_q.shape[3]
    length = context_len[0]
    head_weight = index_weight[0]
    index_rows = index_q[0].reshape(tile_len * index_heads, index_width)
    weight_f32 = head_weight.astype(jnp.float32)
    piece = lax.all_gather(index_keys[0], "ctx", axis=0, tiled=True)
    count = piece.shape[0]
    products = jnp.dot(index_rows, piece.T, preferred_element_type=jnp.float32)
    activ = jnp.maximum(products, 0.0).reshape(tile_len, index_heads, count)
    weighted = jnp.einsum("tjr,tj->tr", activ, weight_f32, precision=lax.Precision.HIGHEST)
    positions = jnp.arange(count)
    weighted = jnp.where(positions[None, :] < length, weighted, 0.0)
    summed = jax.ops.segment_sum(weighted.T, positions // BLK, num_segments=block_total)
    block_sums = summed.T
    block_score = (block_sums / BLK).reshape(1, tile_len, block_total)
    all_lists = lax.all_gather(block_list[0], "ctx", axis=0, tiled=True)
    is_mine = all_lists // blocks_dev == my_index
    slot_index = jnp.sum(jnp.where(is_mine, all_lists % blocks_dev, 0), axis=1)
    wanted = jnp.any(is_mine, axis=1)
    own_blocks = kv_cache[0].reshape(blocks_dev, BLK, row_width)
    outgoing = jnp.where(wanted[:, None, None], own_blocks[slot_index], jnp.zeros((), jnp.bfloat16))
    incoming = lax.all_to_all(outgoing, "ctx", split_axis=0, concat_axis=0, tiled=True)
    chosen = block_list[0, 0]
    cached_rows = incoming[chosen // blocks_dev].reshape(-1, row_width)
    positions = (chosen[:, None] * BLK + jnp.arange(BLK)[None, :]).reshape(-1)
    key_rows = jnp.concatenate([cached_rows, kv_new[0]], axis=0)
    query_rows = q_latent[0].reshape(tile_len * head_count, row_width)
    scores = jnp.dot(query_rows, key_rows.T, preferred_element_type=jnp.float32) * softmax_scale
    cache_ok = positions < length
    token_of = jnp.arange(tile_len * head_count) // head_count
    new_ok = jnp.arange(tile_len)[None, :] <= token_of[:, None]
    allowed = jnp.concatenate(
        [
            jnp.broadcast_to(cache_ok[None, :], (tile_len * head_count, cached_rows.shape[0])),
            new_ok,
        ],
        axis=1,
    )
    scores = jnp.where(allowed, scores, neg_fill)
    highest = jnp.max(scores, axis=1, keepdims=True)
    expo = jnp.exp(scores - highest)
    total = jnp.sum(expo, axis=1, keepdims=True)
    probs = expo.astype(jnp.bfloat16)
    mixed = jnp.dot(probs, key_rows[:, :latent_width], preferred_element_type=jnp.float32) / total
    attended = mixed.astype(jnp.bfloat16).reshape(1, tile_len, head_count, latent_width)
    return (attended, block_score)


def solution(mesh):
    placed = (
        P(("groups", "batch"), "ctx", None, None),
        P(("groups", "batch"), "ctx", None),
        P(("groups", "batch"), "ctx", None),
        P(("groups", "batch"), "ctx", None, None),
        P(("groups", "batch"), "ctx", None),
        P(("groups", "batch"), "ctx", None),
        P(("groups", "batch"), "ctx", None),
        P(("groups", "batch")),
    )
    return jax.shard_map(
        on_ring if mesh.shape["ctx"] == 8 and mesh.shape["batch"] == 2 else on_device,
        mesh=mesh,
        in_specs=placed,
        out_specs=(P(("groups", "batch"), "ctx", None, None), P(("groups", "batch"), "ctx", None)),
        check_vma=False,
    )
```

```python
import functools
import math

import jax
import jax.numpy as jnp
from jax import lax
from jax.experimental import pallas as pl
from jax.experimental.pallas import tpu as pltpu
from jax.sharding import PartitionSpec as P

DR = 64
BLK = 64


softmax_scale = 0.07216878364870322
neg_fill = -1e30
F32 = jnp.float32
BF16 = jnp.bfloat16


def nt_dot(a, b):
    return lax.dot_general(a, b, (((1,), (1,)), ((), ())), preferred_element_type=F32)


def turn(x):
    return jnp.concatenate([x[:, BLK:], x[:, :BLK]], axis=1)


RING = (0, 2, 3, 1)


def ring_steps(me):
    level = me // 2
    odd = jnp.bitwise_xor(level, level // 2) % 2 != lax.axis_index("batch")
    return jnp.where(odd, 4, 2), jnp.where(odd, 2, 4), 6


def pick_kernel(step, width, top, list_ref, line_ref, out_ref):
    me = lax.axis_index("ctx")
    holder = jnp.bitwise_xor(me, ring_steps(me)[step])
    asked = jnp.where(list_ref[...] == 2 * holder + 1, 1.0, 0.0)
    upper = jnp.max(asked, axis=1, keepdims=True) > 0.5
    low = width - top
    rows = 2 * BLK
    lane = lax.broadcasted_iota(jnp.int32, (1, rows), 1)
    first = line_ref[0:low, :].astype(F32)
    second = line_ref[top:width, :].astype(F32)
    first = jnp.where(upper, turn(first), first)
    second = jnp.where(upper, second, turn(second))
    out_ref[0:low, :] = jnp.where(lane < BLK, first, second).astype(BF16)
    out_ref[low : low + rows, :] = line_ref[width : width + rows, :]


def prepare_kernel(q_ref, new_ref, rows_ref, scores_ref, new_rows_ref, wide_ref):
    tokens, _, heads = q_ref.shape
    padding = jnp.zeros((wide_ref.shape[0] - tokens, wide_ref.shape[1]), F32)
    wide = jnp.concatenate([new_ref[...].astype(F32), padding], axis=0).astype(BF16)
    wide_ref[...] = wide
    new_rows_ref[...] = wide[:, 0 : new_rows_ref.shape[1]]
    column = lax.broadcasted_iota(jnp.int32, (1, wide_ref.shape[0]), 1)
    for t in range(tokens):
        rows_ref[t * heads : (t + 1) * heads, :] = q_ref[t].T
    scores = nt_dot(rows_ref[...], wide_ref[...])
    for t in range(tokens):
        place = slice(t * heads, (t + 1) * heads)
        scores_ref[place, :] = jnp.where(column <= t, scores[place, :], neg_fill)


def page_sums(keys, query, room, holder, sums):
    rows = 2 * BLK
    row = lax.broadcasted_iota(jnp.int32, (rows, rows), 0)
    keys = jnp.where(row < room, keys, jnp.zeros((), BF16))
    activ = jnp.maximum(nt_dot(keys, query), 0.0)
    sums[pl.ds(2 * holder, 1), :] = jnp.sum(activ[0:BLK, :], axis=0, keepdims=True)
    sums[pl.ds(2 * holder + 1, 1), :] = jnp.sum(activ[BLK:rows, :], axis=0, keepdims=True)


def weigh(weight_ref, sums):
    weight = weight_ref[...].astype(F32)
    tokens, heads = weight.shape
    total = sums.shape[1]
    lane = lax.broadcasted_iota(jnp.int32, (tokens, total), 1)
    token = lax.broadcasted_iota(jnp.int32, (tokens, total), 0)
    wide = jnp.where(lane // heads == token, jnp.concatenate([weight] * tokens, axis=1), 0.0)
    score = lax.dot_general(
        wide, sums[...], (((1,), (1,)), ((), ())), precision=lax.Precision.HIGHEST, preferred_element_type=F32
    )
    return score * (1.0 / BLK)


def early_kernel(
    width, latent, top, list_ref, length_ref, weight_ref, query_ref,
    own, near, below, above, far, side_below, side_above,
    score_ref, turned_ref, rows_ref, marks_ref, slots, sums,
):
    me = lax.axis_index("ctx")
    behind, ahead, opposite = ring_steps(me)
    last = jnp.bitwise_xor(me, opposite + 1)
    low = width - top
    rows = 2 * BLK
    lane = lax.broadcasted_iota(jnp.int32, (1, rows), 1)
    for slot, ref in ((0, own), (1, near), (behind, below), (ahead, above), (opposite, far)):
        slots[slot] = ref[0:width, :]
    for slot, ref in ((behind + 1, side_below), (ahead + 1, side_above)):
        slots[slot, 0:top, :] = ref[0:top, :]
        slots[slot, top:width, :] = turn(ref[0:low, :].astype(F32)).astype(BF16)
    slots[opposite + 1] = jnp.zeros((width, rows), BF16)
    column = lax.broadcasted_iota(jnp.int32, (1, list_ref.shape[0] * BLK), 1)
    limit = jnp.zeros_like(column)
    late = jnp.zeros_like(column)
    length = length_ref[0]
    pages = list_ref.shape[0]
    for pair in range(pages // 2):
        halves = []
        for j in (2 * pair, 2 * pair + 1):
            page = list_ref[j]
            holder, half = page // 2, lax.rem(page, 2)
            slot = jnp.bitwise_xor(holder, me)
            high = jnp.where((slot == 1) | (lax.rem(slot, 2) == 0), half, 0)
            block = slots[slot].astype(F32)
            halves.append(jnp.where(high == j - 2 * pair, block, turn(block)))
            limit = jnp.where(column // BLK == j, length - page * BLK + j * BLK, limit)
            late = jnp.where((column // BLK == j) & (holder == last), 1, late)
        block = jnp.where(lane < BLK, halves[0], halves[1]).astype(BF16)
        place = slice(pair * rows, (pair + 1) * rows)
        turned_ref[:, place] = block
        rows_ref[place, :] = block[0:latent, :].T
    marks_ref[0:1, :] = limit
    marks_ref[1:2, :] = late
    marks_ref[2:3, :] = jnp.full_like(column, length - last * rows)
    query = query_ref[...]
    sums[pl.ds(2 * last, 1), :] = jnp.zeros((1, sums.shape[1]), F32)
    sums[pl.ds(2 * last + 1, 1), :] = jnp.zeros((1, sums.shape[1]), F32)
    for ref, start, step in (
        (own, width, 0),
        (near, width, 1),
        (below, width, behind),
        (above, width, ahead),
        (far, width, opposite),
        (side_below, low, behind + 1),
        (side_above, low, ahead + 1),
    ):
        holder = jnp.bitwise_xor(me, step)
        page_sums(ref[start : start + rows, :], query, length - holder * rows, holder, sums)
    score_ref[...] = weigh(weight_ref, sums)


def attend_kernel(
    width, latent, top, chunk, q_ref, fresh_ref, new_rows, early_turned, early_rows, marks_ref, early_score, side_far,
    weight_ref, query_ref,
    out_hbm, score_hbm, turned, key_rows, sums, out_ref, score_ref, sems,
):
    last = jnp.bitwise_xor(lax.axis_index("ctx"), 7)
    low = width - top
    rows = 2 * BLK
    sums[...] = jnp.zeros_like(sums)
    page_sums(side_far[low : low + rows, :], query_ref[...], marks_ref[2:3, 0:rows], last, sums)
    score_ref[...] = early_score[...] + weigh(weight_ref, sums)
    steps = q_ref.shape[0] // chunk
    copies = [pltpu.make_async_copy(score_ref, score_hbm, sems.at[steps])]
    copies[0].start()
    lane = lax.broadcasted_iota(jnp.int32, (1, rows), 1)
    packed = side_far[0:low, :].astype(F32)
    swapped = turn(packed)
    first = jnp.concatenate([packed[0:top], swapped], axis=0)
    second = jnp.concatenate([swapped[0:top], packed], axis=0)
    both = jnp.where(lane < BLK, first, second).astype(BF16)
    both_rows = both[0:latent, :].T
    limit = marks_ref[0:1, :]
    late = marks_ref[1:2, :]
    for place in range(0, turned.shape[1], rows):
        place = slice(place, place + rows)
        turned[:, place] = jnp.where(late[:, place] == 1, both, early_turned[:, place])
        down = jnp.broadcast_to(late[:, place].astype(F32), (rows, rows)).T[:, 0:1]
        key_rows[place, :] = jnp.where(down > 0.5, both_rows, early_rows[place, :])
    factor = softmax_scale * math.log2(math.e)
    column = lax.broadcasted_iota(jnp.int32, (1, turned.shape[1]), 1)
    for step in range(steps):
        place = slice(step * chunk, (step + 1) * chunk)
        scores = jnp.dot(q_ref[place, :], turned[...], preferred_element_type=F32)
        scores = jnp.where(column < limit, scores, neg_fill)
        fresh = fresh_ref[place, :]
        highest = jnp.maximum(jnp.max(scores, axis=1, keepdims=True), jnp.max(fresh, axis=1, keepdims=True))
        expo = jnp.exp2((scores - highest) * factor)
        expo_new = jnp.exp2((fresh - highest) * factor)
        total = jnp.sum(expo, axis=1, keepdims=True) + jnp.sum(expo_new, axis=1, keepdims=True)
        probs = jnp.concatenate([expo.astype(BF16), expo_new.astype(BF16)], axis=1)
        values = jnp.concatenate([key_rows[...], new_rows[...]], axis=0)
        mixed = jnp.dot(probs, values, preferred_element_type=F32)
        out_ref[place, :] = (mixed / total).astype(BF16)
        copies.append(pltpu.make_async_copy(out_ref.at[place], out_hbm.at[place], sems.at[step]))
        copies[-1].start()
    for copy in copies:
        copy.wait()


VMEM = pl.BlockSpec(memory_space=pltpu.VMEM)
SMEM = pl.BlockSpec(memory_space=pltpu.SMEM)
ANY = pl.BlockSpec(memory_space=pl.ANY)


def call(body, shapes, in_specs, out_specs=VMEM, scratch=(), moved=0):
    return pl.pallas_call(
        body,
        out_shape=shapes,
        in_specs=in_specs,
        out_specs=out_specs,
        scratch_shapes=scratch,
        cost_estimate=pl.CostEstimate(flops=0, bytes_accessed=moved, transcendentals=0),
        compiler_params=pltpu.CompilerParams(vmem_limit_bytes=32 * 1024 * 1024),
    )


def on_ring(
    q_latent, kv_new, kv_cache, index_q, index_weight, index_keys, block_list, context_len
):
    count = lax.axis_size("ctx")
    tile_len, head_count, width = q_latent.shape[1:]
    latent = width - DR
    rows = kv_cache.shape[1]
    chosen = block_list[0, 0]
    top = width // 2
    low = width - top
    pages = kv_cache[0].T
    query = jnp.transpose(q_latent[0], (0, 2, 1))
    shape = jax.ShapeDtypeStruct

    def shift(x, by):
        places = len(RING)
        pairs = [
            ((RING[p] * 2 + i) * 2 + core, (RING[(p + (1 - 2 * core) * by) % places] * 2 + i) * 2 + core)
            for p in range(places)
            for i in range(2)
            for core in range(2)
        ]
        return lax.ppermute(x, ("ctx", "batch"), pairs)

    def swap(x):
        return lax.ppermute(x, "ctx", [(i, i ^ 1) for i in range(count)])

    def pick(step, line):
        body = functools.partial(pick_kernel, step, width, top)
        return call(body, shape((low + rows, rows), BF16), [VMEM] * 2, moved=10**7)(asked, line)

    own = jnp.concatenate([pages, index_keys[0]], axis=0)
    below = shift(own, 1)
    near = swap(own)
    above = shift(own, -1)
    asked = swap(block_list[0])
    query_count = tile_len * head_count
    index_rows = index_q[0].reshape(-1, index_q.shape[3])
    q_rows, fresh, new_rows = call(
        prepare_kernel,
        (shape((query_count, width), BF16), shape((query_count, 128), F32), shape((128, latent), BF16)),
        [VMEM] * 2,
        (VMEM,) * 3,
        [pltpu.VMEM((128, width), BF16)],
        moved=4 * query_count * width,
    )(query, kv_new[0])
    below, asked, q_rows, fresh = lax.optimization_barrier((below, asked, q_rows, fresh))
    far = shift(below, 1)
    asked, near = lax.optimization_barrier((asked, near))
    side_below = swap(pick(0, below))
    side_far = swap(pick(2, far))
    side_above = swap(pick(1, above))
    sums = pltpu.VMEM((2 * count, index_rows.shape[0]), F32)
    columns = chosen.shape[0] * BLK
    score, turned, key_rows, marks = call(
        functools.partial(early_kernel, width, latent, top),
        (shape((tile_len, 2 * count), F32), shape((width, columns), BF16), shape((columns, latent), BF16), shape((8, columns), jnp.int32)),
        [SMEM] * 2 + [VMEM] * 9,
        (VMEM,) * 4,
        [pltpu.VMEM((8, width, rows), BF16), sums],
        moved=4 * query_count * width,
    )(chosen, context_len, index_weight[0], index_rows, own, near, below, above, far, side_below, side_above)
    chunk = query_count // 2
    attended, block_score = call(
        functools.partial(attend_kernel, width, latent, top, chunk),
        (shape((query_count, latent), BF16), shape((tile_len, 2 * count), F32)),
        [VMEM] * 10,
        (ANY, ANY),
        [
            pltpu.VMEM((width, columns), BF16),
            pltpu.VMEM((columns, latent), BF16),
            sums,
            pltpu.VMEM((query_count, latent), BF16),
            pltpu.VMEM((tile_len, 2 * count), F32),
            pltpu.SemaphoreType.DMA((3,)),
        ],
    )(q_rows, fresh, new_rows, turned, key_rows, marks, score, side_far, index_weight[0], index_rows)
    return attended.reshape(1, tile_len, head_count, latent), block_score[None]


def on_device(
    q_latent, kv_new, kv_cache, index_q, index_weight, index_keys, block_list, context_len
):
    ctx_count = lax.axis_size("ctx")
    my_index = lax.axis_index("ctx")
    tile_len = q_latent.shape[1]
    head_count = q_latent.shape[2]
    row_width = q_latent.shape[3]
    latent_width = row_width - DR
    ctx_rows = kv_cache.shape[1]
    blocks_dev = ctx_rows // BLK
    block_total = blocks_dev * ctx_count
    index_heads = index_q.shape[2]
    index_width = index_q.shape[3]
    length = context_len[0]
    head_weight = index_weight[0]
    index_rows = index_q[0].reshape(tile_len * index_heads, index_width)
    weight_f32 = head_weight.astype(jnp.float32)
    piece = lax.all_gather(index_keys[0], "ctx", axis=0, tiled=True)
    count = piece.shape[0]
    products = jnp.dot(index_rows, piece.T, preferred_element_type=jnp.float32)
    activ = jnp.maximum(products, 0.0).reshape(tile_len, index_heads, count)
    weighted = jnp.einsum("tjr,tj->tr", activ, weight_f32, precision=lax.Precision.HIGHEST)
    positions = jnp.arange(count)
    weighted = jnp.where(positions[None, :] < length, weighted, 0.0)
    summed = jax.ops.segment_sum(weighted.T, positions // BLK, num_segments=block_total)
    block_sums = summed.T
    block_score = (block_sums / BLK).reshape(1, tile_len, block_total)
    all_lists = lax.all_gather(block_list[0], "ctx", axis=0, tiled=True)
    is_mine = all_lists // blocks_dev == my_index
    slot_index = jnp.sum(jnp.where(is_mine, all_lists % blocks_dev, 0), axis=1)
    wanted = jnp.any(is_mine, axis=1)
    own_blocks = kv_cache[0].reshape(blocks_dev, BLK, row_width)
    outgoing = jnp.where(wanted[:, None, None], own_blocks[slot_index], jnp.zeros((), jnp.bfloat16))
    incoming = lax.all_to_all(outgoing, "ctx", split_axis=0, concat_axis=0, tiled=True)
    chosen = block_list[0, 0]
    cached_rows = incoming[chosen // blocks_dev].reshape(-1, row_width)
    positions = (chosen[:, None] * BLK + jnp.arange(BLK)[None, :]).reshape(-1)
    key_rows = jnp.concatenate([cached_rows, kv_new[0]], axis=0)
    query_rows = q_latent[0].reshape(tile_len * head_count, row_width)
    scores = jnp.dot(query_rows, key_rows.T, preferred_element_type=jnp.float32) * softmax_scale
    cache_ok = positions < length
    token_of = jnp.arange(tile_len * head_count) // head_count
    new_ok = jnp.arange(tile_len)[None, :] <= token_of[:, None]
    allowed = jnp.concatenate(
        [
            jnp.broadcast_to(cache_ok[None, :], (tile_len * head_count, cached_rows.shape[0])),
            new_ok,
        ],
        axis=1,
    )
    scores = jnp.where(allowed, scores, neg_fill)
    highest = jnp.max(scores, axis=1, keepdims=True)
    expo = jnp.exp(scores - highest)
    total = jnp.sum(expo, axis=1, keepdims=True)
    probs = expo.astype(jnp.bfloat16)
    mixed = jnp.dot(probs, key_rows[:, :latent_width], preferred_element_type=jnp.float32) / total
    attended = mixed.astype(jnp.bfloat16).reshape(1, tile_len, head_count, latent_width)
    return (attended, block_score)


def solution(mesh):
    placed = (
        P(("groups", "batch"), "ctx", None, None),
        P(("groups", "batch"), "ctx", None),
        P(("groups", "batch"), "ctx", None),
        P(("groups", "batch"), "ctx", None, None),
        P(("groups", "batch"), "ctx", None),
        P(("groups", "batch"), "ctx", None),
        P(("groups", "batch"), "ctx", None),
        P(("groups", "batch")),
    )
    return jax.shard_map(
        on_ring if mesh.shape["ctx"] == 8 and mesh.shape["batch"] == 2 else on_device,
        mesh=mesh,
        in_specs=placed,
        out_specs=(P(("groups", "batch"), "ctx", None, None), P(("groups", "batch"), "ctx", None)),
        check_vma=False,
    )
```

```python
import functools
import math

import jax
import jax.numpy as jnp
from jax import lax
from jax.experimental import pallas as pl
from jax.experimental.pallas import tpu as pltpu
from jax.sharding import PartitionSpec as P

DR = 64
BLK = 64


softmax_scale = 0.07216878364870322
neg_fill = -1e30
F32 = jnp.float32
BF16 = jnp.bfloat16


def nt_dot(a, b):
    return lax.dot_general(a, b, (((1,), (1,)), ((), ())), preferred_element_type=F32)


def turn(x):
    return jnp.concatenate([x[:, BLK:], x[:, :BLK]], axis=1)


RING = (0, 2, 3, 1)


def ring_steps(me):
    level = me // 2
    odd = jnp.bitwise_xor(level, level // 2) % 2 != lax.axis_index("batch")
    return jnp.where(odd, 4, 2), jnp.where(odd, 2, 4), 6


def pick_kernel(step, width, top, list_ref, line_ref, out_ref):
    me = lax.axis_index("ctx")
    holder = jnp.bitwise_xor(me, ring_steps(me)[step])
    asked = jnp.where(list_ref[...] == 2 * holder + 1, 1.0, 0.0)
    upper = jnp.max(asked, axis=1, keepdims=True) > 0.5
    low = width - top
    rows = 2 * BLK
    lane = lax.broadcasted_iota(jnp.int32, (1, rows), 1)
    keep = jnp.logical_xor(lane < BLK, upper)
    first = line_ref[0:low, :].astype(F32)
    second = line_ref[top:width, :].astype(F32)
    first = jnp.where(upper, turn(first), first)
    second = jnp.where(upper, second, turn(second))
    out_ref[0:low, :] = jnp.where(lane < BLK, first, second).astype(BF16)
    out_ref[low : low + rows, :] = line_ref[width : width + rows, :]


def prepare_kernel(q_ref, new_ref, rows_ref, scores_ref, new_rows_ref, wide_ref):
    tokens, _, heads = q_ref.shape
    padding = jnp.zeros((wide_ref.shape[0] - tokens, wide_ref.shape[1]), F32)
    wide = jnp.concatenate([new_ref[...].astype(F32), padding], axis=0).astype(BF16)
    wide_ref[...] = wide
    new_rows_ref[...] = wide[:, 0 : new_rows_ref.shape[1]]
    column = lax.broadcasted_iota(jnp.int32, (1, wide_ref.shape[0]), 1)
    for t in range(tokens):
        rows_ref[t * heads : (t + 1) * heads, :] = q_ref[t].T
    scores = nt_dot(rows_ref[...], wide_ref[...])
    for t in range(tokens):
        place = slice(t * heads, (t + 1) * heads)
        scores_ref[place, :] = jnp.where(column <= t, scores[place, :], neg_fill)


def page_sums(keys, query, room, holder, sums):
    rows = 2 * BLK
    row = lax.broadcasted_iota(jnp.int32, (rows, rows), 0)
    keys = jnp.where(row < room, keys, jnp.zeros((), BF16))
    activ = jnp.maximum(nt_dot(keys, query), 0.0)
    sums[pl.ds(2 * holder, 1), :] = jnp.sum(activ[0:BLK, :], axis=0, keepdims=True)
    sums[pl.ds(2 * holder + 1, 1), :] = jnp.sum(activ[BLK:rows, :], axis=0, keepdims=True)


def weigh(weight_ref, sums):
    weight = weight_ref[...].astype(F32)
    tokens, heads = weight.shape
    total = sums.shape[1]
    lane = lax.broadcasted_iota(jnp.int32, (tokens, total), 1)
    token = lax.broadcasted_iota(jnp.int32, (tokens, total), 0)
    wide = jnp.where(lane // heads == token, jnp.concatenate([weight] * tokens, axis=1), 0.0)
    score = lax.dot_general(
        wide, sums[...], (((1,), (1,)), ((), ())), precision=lax.Precision.HIGHEST, preferred_element_type=F32
    )
    return score * (1.0 / BLK)


def early_kernel(
    width, latent, top, list_ref, length_ref, weight_ref, query_ref,
    own, near, below, above, far, side_below,
    score_ref, turned_ref, rows_ref, marks_ref, slots, sums,
):
    me = lax.axis_index("ctx")
    behind, ahead, opposite = ring_steps(me)
    missing = (jnp.bitwise_xor(me, ahead + 1), jnp.bitwise_xor(me, opposite + 1))
    low = width - top
    rows = 2 * BLK
    lane = lax.broadcasted_iota(jnp.int32, (1, rows), 1)
    for slot, ref in ((0, own), (1, near), (behind, below), (ahead, above), (opposite, far)):
        slots[slot] = ref[0:width, :]
    slots[behind + 1, 0:top, :] = side_below[0:top, :]
    slots[behind + 1, top:width, :] = turn(side_below[0:low, :].astype(F32)).astype(BF16)
    slots[ahead + 1] = jnp.zeros((width, rows), BF16)
    slots[opposite + 1] = jnp.zeros((width, rows), BF16)
    column = lax.broadcasted_iota(jnp.int32, (1, list_ref.shape[0] * BLK), 1)
    limit = jnp.zeros_like(column)
    late = jnp.zeros_like(column)
    length = length_ref[0]
    pages = list_ref.shape[0]
    for pair in range(pages // 2):
        halves = []
        for j in (2 * pair, 2 * pair + 1):
            page = list_ref[j]
            holder, half = page // 2, lax.rem(page, 2)
            slot = jnp.bitwise_xor(holder, me)
            high = jnp.where((slot == 1) | (lax.rem(slot, 2) == 0), half, 0)
            block = slots[slot].astype(F32)
            halves.append(jnp.where(high == j - 2 * pair, block, turn(block)))
            limit = jnp.where(column // BLK == j, length - page * BLK + j * BLK, limit)
            for number, absent in enumerate(missing):
                late = jnp.where((column // BLK == j) & (holder == absent), number + 1, late)
        block = jnp.where(lane < BLK, halves[0], halves[1]).astype(BF16)
        place = slice(pair * rows, (pair + 1) * rows)
        turned_ref[:, place] = block
        rows_ref[place, :] = block[0:latent, :].T
    marks_ref[0:1, :] = limit
    marks_ref[1:2, :] = late
    for number, absent in enumerate(missing):
        marks_ref[number + 2 : number + 3, :] = jnp.full_like(column, length - absent * rows)
        for half in range(2):
            sums[pl.ds(2 * absent + half, 1), :] = jnp.zeros((1, sums.shape[1]), F32)
    query = query_ref[...]
    for ref, start, step in (
        (own, width, 0),
        (near, width, 1),
        (below, width, behind),
        (above, width, ahead),
        (far, width, opposite),
        (side_below, low, behind + 1),
    ):
        holder = jnp.bitwise_xor(me, step)
        page_sums(ref[start : start + rows, :], query, length - holder * rows, holder, sums)
    score_ref[...] = weigh(weight_ref, sums)


def attend_kernel(
    width, latent, top, chunk, q_ref, fresh_ref, new_rows, early_turned, early_rows, marks_ref, early_score, side_above, side_far, weight_ref, query_ref,
    out_hbm, score_hbm, turned, key_rows, sums, out_ref, score_ref, sems,
):
    me = lax.axis_index("ctx")
    low = width - top
    rows = 2 * BLK
    sums[...] = jnp.zeros_like(sums)
    arrived = ((side_above, ring_steps(me)[1] + 1), (side_far, ring_steps(me)[2] + 1))
    for number, (ref, step) in enumerate(arrived):
        room = marks_ref[number + 2 : number + 3, 0:rows]
        page_sums(ref[low : low + rows, :], query_ref[...], room, jnp.bitwise_xor(me, step), sums)
    score_ref[...] = early_score[...] + weigh(weight_ref, sums)
    steps = q_ref.shape[0] // chunk
    copies = [pltpu.make_async_copy(score_ref, score_hbm, sems.at[steps])]
    copies[0].start()
    lane = lax.broadcasted_iota(jnp.int32, (1, rows), 1)
    limit = marks_ref[0:1, :]
    late = marks_ref[1:2, :]
    turned[...] = early_turned[...]
    key_rows[...] = early_rows[...]
    for number, (ref, _) in enumerate(arrived):
        packed = ref[0:low, :].astype(F32)
        swapped = turn(packed)
        first = jnp.concatenate([packed[0:top], swapped], axis=0)
        second = jnp.concatenate([swapped[0:top], packed], axis=0)
        both = jnp.where(lane < BLK, first, second).astype(BF16)
        both_rows = both[0:latent, :].T
        for place in range(0, turned.shape[1], rows):
            place = slice(place, place + rows)
            here = late[:, place] == number + 1
            turned[:, place] = jnp.where(here, both, turned[:, place])
            down = jnp.broadcast_to(jnp.where(here, 1.0, 0.0), (rows, rows)).T[:, 0:1]
            key_rows[place, :] = jnp.where(down > 0.5, both_rows, key_rows[place, :])
    factor = softmax_scale * math.log2(math.e)
    column = lax.broadcasted_iota(jnp.int32, (1, turned.shape[1]), 1)
    for step in range(steps):
        place = slice(step * chunk, (step + 1) * chunk)
        scores = jnp.dot(q_ref[place, :], turned[...], preferred_element_type=F32)
        scores = jnp.where(column < limit, scores, neg_fill)
        fresh = fresh_ref[place, :]
        highest = jnp.maximum(jnp.max(scores, axis=1, keepdims=True), jnp.max(fresh, axis=1, keepdims=True))
        expo = jnp.exp2((scores - highest) * factor)
        expo_new = jnp.exp2((fresh - highest) * factor)
        total = jnp.sum(expo, axis=1, keepdims=True) + jnp.sum(expo_new, axis=1, keepdims=True)
        probs = jnp.concatenate([expo.astype(BF16), expo_new.astype(BF16)], axis=1)
        values = jnp.concatenate([key_rows[...], new_rows[...]], axis=0)
        mixed = jnp.dot(probs, values, preferred_element_type=F32)
        out_ref[place, :] = (mixed / total).astype(BF16)
        copies.append(pltpu.make_async_copy(out_ref.at[place], out_hbm.at[place], sems.at[step]))
        copies[-1].start()
    for copy in copies:
        copy.wait()


VMEM = pl.BlockSpec(memory_space=pltpu.VMEM)
SMEM = pl.BlockSpec(memory_space=pltpu.SMEM)


ANY = pl.BlockSpec(memory_space=pl.ANY)


def call(body, shapes, in_specs, out_specs=VMEM, scratch=(), flops=0, moved=0, vmem=32):
    return pl.pallas_call(
        body,
        out_shape=shapes,
        in_specs=in_specs,
        out_specs=out_specs,
        scratch_shapes=scratch,
        cost_estimate=pl.CostEstimate(flops=flops, bytes_accessed=moved, transcendentals=0),
        compiler_params=pltpu.CompilerParams(vmem_limit_bytes=vmem * 1024 * 1024),
    )


def on_ring(
    q_latent, kv_new, kv_cache, index_q, index_weight, index_keys, block_list, context_len
):
    count = lax.axis_size("ctx")
    tile_len, head_count, width = q_latent.shape[1:]
    latent = width - DR
    rows = kv_cache.shape[1]
    chosen = block_list[0, 0]
    top = width // 2
    low = width - top
    pages = kv_cache[0].T
    query = jnp.transpose(q_latent[0], (0, 2, 1))
    shape = jax.ShapeDtypeStruct

    def shift(x, by):
        places = len(RING)
        pairs = [
            ((RING[p] * 2 + i) * 2 + core, (RING[(p + (1 - 2 * core) * by) % places] * 2 + i) * 2 + core)
            for p in range(places)
            for i in range(2)
            for core in range(2)
        ]
        return lax.ppermute(x, ("ctx", "batch"), pairs)

    def swap(x):
        return lax.ppermute(x, "ctx", [(i, i ^ 1) for i in range(count)])

    def pick(step, line):
        body = functools.partial(pick_kernel, step, width, top)
        return call(body, shape((low + rows, rows), BF16), [VMEM] * 2, moved=10**7)(asked, line)

    own = jnp.concatenate([pages, index_keys[0]], axis=0)
    below = shift(own, 1)
    near = swap(own)
    above = shift(own, -1)
    asked = swap(block_list[0])
    query_count = tile_len * head_count
    index_rows = index_q[0].reshape(-1, index_q.shape[3])
    q_rows, fresh, new_rows = call(
        prepare_kernel,
        (shape((query_count, width), BF16), shape((query_count, 128), F32), shape((128, latent), BF16)),
        [VMEM] * 2,
        (VMEM,) * 3,
        [pltpu.VMEM((128, width), BF16)],
        moved=4 * query_count * width,
    )(query, kv_new[0])
    below, asked, q_rows, fresh = lax.optimization_barrier((below, asked, q_rows, fresh))
    far = shift(below, 1)
    asked, near = lax.optimization_barrier((asked, near))
    side_below = swap(pick(0, below))
    side_far = swap(pick(2, far))
    side_above = swap(pick(1, above))
    sums = pltpu.VMEM((2 * count, index_rows.shape[0]), F32)
    columns = chosen.shape[0] * BLK
    score, turned, key_rows, marks = call(
        functools.partial(early_kernel, width, latent, top),
        (shape((tile_len, 2 * count), F32), shape((width, columns), BF16), shape((columns, latent), BF16), shape((8, columns), jnp.int32)),
        [SMEM] * 2 + [VMEM] * 8,
        (VMEM,) * 4,
        [pltpu.VMEM((8, width, rows), BF16), sums],
        moved=4 * query_count * width,
    )(chosen, context_len, index_weight[0], index_rows, own, near, below, above, far, side_below)
    chunk = query_count // 2
    attended, block_score = call(
        functools.partial(attend_kernel, width, latent, top, chunk),
        (shape((query_count, latent), BF16), shape((tile_len, 2 * count), F32)),
        [VMEM] * 11,
        (ANY, ANY),
        [
            pltpu.VMEM((width, columns), BF16),
            pltpu.VMEM((columns, latent), BF16),
            sums,
            pltpu.VMEM((query_count, latent), BF16),
            pltpu.VMEM((tile_len, 2 * count), F32),
            pltpu.SemaphoreType.DMA((2 + 1,)),
        ],
    )(q_rows, fresh, new_rows, turned, key_rows, marks, score, side_above, side_far, index_weight[0], index_rows)
    return attended.reshape(1, tile_len, head_count, latent), block_score[None]


def on_device(
    q_latent, kv_new, kv_cache, index_q, index_weight, index_keys, block_list, context_len
):
    ctx_count = lax.axis_size("ctx")
    my_index = lax.axis_index("ctx")
    tile_len = q_latent.shape[1]
    head_count = q_latent.shape[2]
    row_width = q_latent.shape[3]
    latent_width = row_width - DR
    ctx_rows = kv_cache.shape[1]
    blocks_dev = ctx_rows // BLK
    block_total = blocks_dev * ctx_count
    index_heads = index_q.shape[2]
    index_width = index_q.shape[3]
    length = context_len[0]
    head_weight = index_weight[0]
    index_rows = index_q[0].reshape(tile_len * index_heads, index_width)
    weight_f32 = head_weight.astype(jnp.float32)
    piece = lax.all_gather(index_keys[0], "ctx", axis=0, tiled=True)
    count = piece.shape[0]
    products = jnp.dot(index_rows, piece.T, preferred_element_type=jnp.float32)
    activ = jnp.maximum(products, 0.0).reshape(tile_len, index_heads, count)
    weighted = jnp.einsum("tjr,tj->tr", activ, weight_f32, precision=lax.Precision.HIGHEST)
    positions = jnp.arange(count)
    weighted = jnp.where(positions[None, :] < length, weighted, 0.0)
    summed = jax.ops.segment_sum(weighted.T, positions // BLK, num_segments=block_total)
    block_sums = summed.T
    block_score = (block_sums / BLK).reshape(1, tile_len, block_total)
    all_lists = lax.all_gather(block_list[0], "ctx", axis=0, tiled=True)
    is_mine = all_lists // blocks_dev == my_index
    slot_index = jnp.sum(jnp.where(is_mine, all_lists % blocks_dev, 0), axis=1)
    wanted = jnp.any(is_mine, axis=1)
    own_blocks = kv_cache[0].reshape(blocks_dev, BLK, row_width)
    outgoing = jnp.where(wanted[:, None, None], own_blocks[slot_index], jnp.zeros((), jnp.bfloat16))
    incoming = lax.all_to_all(outgoing, "ctx", split_axis=0, concat_axis=0, tiled=True)
    chosen = block_list[0, 0]
    cached_rows = incoming[chosen // blocks_dev].reshape(-1, row_width)
    positions = (chosen[:, None] * BLK + jnp.arange(BLK)[None, :]).reshape(-1)
    key_rows = jnp.concatenate([cached_rows, kv_new[0]], axis=0)
    query_rows = q_latent[0].reshape(tile_len * head_count, row_width)
    scores = jnp.dot(query_rows, key_rows.T, preferred_element_type=jnp.float32) * softmax_scale
    cache_ok = positions < length
    token_of = jnp.arange(tile_len * head_count) // head_count
    new_ok = jnp.arange(tile_len)[None, :] <= token_of[:, None]
    allowed = jnp.concatenate(
        [
            jnp.broadcast_to(cache_ok[None, :], (tile_len * head_count, cached_rows.shape[0])),
            new_ok,
        ],
        axis=1,
    )
    scores = jnp.where(allowed, scores, neg_fill)
    highest = jnp.max(scores, axis=1, keepdims=True)
    expo = jnp.exp(scores - highest)
    total = jnp.sum(expo, axis=1, keepdims=True)
    probs = expo.astype(jnp.bfloat16)
    mixed = jnp.dot(probs, key_rows[:, :latent_width], preferred_element_type=jnp.float32) / total
    attended = mixed.astype(jnp.bfloat16).reshape(1, tile_len, head_count, latent_width)
    return (attended, block_score)


def solution(mesh):
    placed = (
        P(("groups", "batch"), "ctx", None, None),
        P(("groups", "batch"), "ctx", None),
        P(("groups", "batch"), "ctx", None),
        P(("groups", "batch"), "ctx", None, None),
        P(("groups", "batch"), "ctx", None),
        P(("groups", "batch"), "ctx", None),
        P(("groups", "batch"), "ctx", None),
        P(("groups", "batch")),
    )
    return jax.shard_map(
        on_ring if mesh.shape["ctx"] == 8 and mesh.shape["batch"] == 2 else on_device,
        mesh=mesh,
        in_specs=placed,
        out_specs=(P(("groups", "batch"), "ctx", None, None), P(("groups", "batch"), "ctx", None)),
        check_vma=False,
    )
```
